128 devices in a mesh: gx: 16 (over x_hi, y, core), gy: 8 (over x_lo, z).
Axes of the slice: x: 4 (x_hi: 2, x_lo: 2; x = x_hi * 2 + x_lo), y: 4, z: 4, core: 2. Of those that a mesh axis runs over, the one named last changes fastest.
Arguments:
- flow_field: bfloat16 [4, 64, 1024, 512], P(None, None, ('gx', 'gy')), may hold values from -6 to 6
- cotangent: bfloat16 [4, 64, 1024, 512], P(None, None, ('gx', 'gy')), may hold values from -2 to 2
- spectral_weight: bfloat16 [128, 64, 64, 128], P(('gx', 'gy')), may hold values from -0.75 to 0.75
- local_weight: bfloat16 [64, 64], replicated, may hold values from -0.75 to 0.75
- channel_bias: float32 [64], replicated, may hold values from -3 to 3
Outputs:
- output_field: bfloat16 [4, 64, 1024, 512], P(None, None, ('gx', 'gy'))
- grad_field: bfloat16 [4, 64, 1024, 512], P(None, None, ('gx', 'gy'))
- grad_spectral: float32 [128, 64, 64, 128], P(('gx', 'gy'))
The draws below stay inside these ranges and needn't reach their ends.
All inputs are finite; a program needn't handle non-finite values.
Results may differ from the reference program's by a relative error of at most 0.014.
Values may be sent and summed in bfloat16 or wider, within the bound.
No kernel may reach another device: no remote copies, remote signals or barrier semaphores. Data moves between devices by JAX's collectives and lax.ppermute only.
A program may use at most 64 MiB of HBM per device.

```python
import math
import jax
import jax.numpy as jnp
from jax import lax

C = 64
NX = 1024
NY = 512
MODES = 64
Z = 4
KC = 128


def level_of(stream_key, dims, cuts, low, high):
    level, own = 1.0, jax.random.fold_in(stream_key, 6)
    for axis_at, blocks in cuts:
        draws = jnp.exp(jax.random.uniform(jax.random.fold_in(own, axis_at), (blocks,), jnp.float32, low / len(cuts), high / len(cuts)))
        level = level * jnp.repeat(draws, dims[axis_at] // blocks).reshape([-1 if axis == axis_at else 1 for axis in range(len(dims))])
    return level


def centred(key, shape, width, bound, cuts=(), kind=jnp.bfloat16):
    factor_of = level_of(key, shape, cuts, -0.22, 0.18) if cuts else 1.0
    values = jax.random.normal(key, shape, jnp.float32) * width * factor_of
    return jnp.minimum(jnp.maximum(values, -bound), bound).astype(kind)


def setup_inputs(seed: int = 0) -> dict:
    splits = jax.random.split(jax.random.key(seed), 6)
    flow_field = centred(splits[0], (Z, C, NX, NY), 1.0, 6.0, ((2, 128),))
    cotangent = centred(splits[1], (Z, C, NX, NY), 0.3, 2.0, ((2, 128),))
    spectral_weight = centred(splits[2], (KC, C, C, KC), C ** -0.5, 0.75, ((0, 128),))
    local_weight = centred(splits[3], (C, C), C ** -0.5, 0.75)
    channel_bias = centred(splits[4], (C,), 0.5, 3.0, (), jnp.float32)
    return dict(flow_field=flow_field, cotangent=cotangent, spectral_weight=spectral_weight, local_weight=local_weight, channel_bias=channel_bias)


root_half = 0.7071067811865476
density_norm = 0.3989422804014327

def basis_table(positions, columns, cells, kept, factor):
    frequency = jnp.where(columns < kept, columns, columns - kept + 1)
    phases = positions[:, None] * frequency[None, :] % cells
    angles = phases.astype(jnp.float32) * (2.0 * math.pi / cells)
    values = jnp.where(columns[None, :] < kept, jnp.cos(angles), jnp.sin(angles))
    return (values * factor).astype(jnp.bfloat16)

def gelu_slope(values):
    cumulative = 0.5 * (1.0 + lax.erf(values * root_half))
    density = jnp.exp(-0.5 * values * values) * density_norm
    return cumulative + values * density

def reference(flow_field, cotangent, spectral_weight, local_weight, channel_bias):
    columns = jnp.arange(2 * MODES, dtype=jnp.int32)
    rows_x = jnp.arange(NX, dtype=jnp.int32)
    rows_y = jnp.arange(NY, dtype=jnp.int32)
    fwd_x = basis_table(rows_x, columns, NX, MODES, math.sqrt(2.0 / NX)).astype(jnp.float32)
    fwd_y = basis_table(rows_y, columns, NY, MODES, math.sqrt(2.0 / NY)).astype(jnp.float32)
    inv_x = basis_table(rows_x, columns, NX, MODES, math.sqrt(1.0 / MODES)).astype(jnp.float32)
    inv_y = basis_table(rows_y, columns, NY, MODES, math.sqrt(1.0 / MODES)).astype(jnp.float32)
    weights = spectral_weight.astype(jnp.float32)
    mixing = local_weight.astype(jnp.float32)

    def to_modes(plane, table_x, table_y):
        along = jnp.einsum('cxy,yj->cjx', plane.astype(jnp.float32), table_y).astype(jnp.bfloat16)
        return jnp.einsum('cjx,xk->cjk', along.astype(jnp.float32), table_x).astype(jnp.bfloat16)

    def to_space(modal, table_x, table_y):
        partial_x = jnp.einsum('cjk,xk->cjx', modal.astype(jnp.float32), table_x).astype(jnp.bfloat16)
        return jnp.einsum('cjx,yj->cxy', partial_x.astype(jnp.float32), table_y, precision=lax.Precision.HIGHEST)

    def plane_step(accum, inputs):
        plane, grad_out = inputs
        coeffs = to_modes(plane, fwd_x, fwd_y)
        mixed = jnp.einsum('ijk,jiok->ojk', coeffs.astype(jnp.float32), weights).astype(jnp.bfloat16)
        spectral = to_space(mixed, inv_x, inv_y)
        pointwise = jnp.einsum('ixy,io->oxy', plane.astype(jnp.float32), mixing)
        pre_activation = spectral + pointwise + channel_bias[:, None, None]
        output_plane = jax.nn.gelu(pre_activation, approximate=False).astype(jnp.bfloat16)
        grad_pre = (grad_out.astype(jnp.float32) * gelu_slope(pre_activation)).astype(jnp.bfloat16)
        grad_mixed = to_modes(grad_pre, inv_x, inv_y)
        accum = accum + jnp.einsum('ijk,ojk->jiok', coeffs.astype(jnp.float32), grad_mixed.astype(jnp.float32))
        grad_coeffs = jnp.einsum('ojk,jiok->ijk', grad_mixed.astype(jnp.float32), weights).astype(jnp.bfloat16)
        backward = to_space(grad_coeffs, fwd_x, fwd_y)
        grad_plane = (backward + jnp.einsum('oxy,io->ixy', grad_pre.astype(jnp.float32), mixing)).astype(jnp.bfloat16)
        return (accum, (output_plane, grad_plane))
    start = jnp.zeros((2 * MODES, C, C, 2 * MODES), jnp.float32)
    grad_spectral, (output_field, grad_field) = lax.scan(plane_step, start, (flow_field, cotangent))
    return (output_field, grad_field, grad_spectral)
```

```python
import functools
import math

import jax
import jax.numpy as jnp
import numpy as np
from jax import lax
from jax.experimental import pallas as pl
from jax.experimental.pallas import tpu as pltpu
from jax.sharding import PartitionSpec as P

AXES = ("gx", "gy")
LANES = 128
VMEM_LIMIT = 28 * 1024 * 1024

TAIL_SHIFT = 0.3
TAIL = (
    0.11962930113077164,
    0.1207539513707161,
    0.09991350024938583,
    0.1285616159439087,
    -0.053683627396821976,
    0.20635350048542023,
    -0.1572030931711197,
    0.03567477688193321,
)
HALF_LOG2E = 0.5 * math.log2(math.e)
DENSITY = 0.3989422804014327


def basis_table(cells, kept, factor):
    positions = np.arange(cells, dtype=np.int64)
    columns = np.arange(2 * kept, dtype=np.int64)
    frequency = np.where(columns < kept, columns, columns - kept + 1)
    phases = positions[:, None] * frequency[None, :] % cells
    angles = phases.astype(np.float32) * np.float32(2.0 * math.pi / cells)
    values = np.where(columns[None, :] < kept, np.cos(angles), np.sin(angles))
    return (values * np.float32(factor)).astype(jnp.bfloat16)


def dot(a, b, contract):
    return lax.dot_general(a, b, (contract, ((), ())), preferred_element_type=jnp.float32)


def params():
    return pltpu.CompilerParams(vmem_limit_bytes=VMEM_LIMIT)


def rows_to_blocks(rows, half, slab, by_rows, by_peer):
    tiles = 2 * slab
    by_rows[...] = rows
    for x in range(slab):
        part = by_rows[pl.ds(x, LANES, stride=slab), :]
        by_peer[pl.ds(half * slab + x, LANES, stride=tiles), :] = part.T


def blocks_to_rows(blocks_ref, slab, by_peer, by_rows):
    tiles = 2 * slab
    by_peer[...] = blocks_ref[...].astype(jnp.float32)
    for half in range(2):
        for x in range(slab):
            part = by_peer[pl.ds(half * slab + x, LANES, stride=tiles), :]
            by_rows[pl.ds(half * LANES * slab + x, LANES, stride=slab), :] = part.T


def analysis_kernel(slab, field_ref, table_ref, out_ref, by_rows, by_peer):
    half = pl.program_id(0)
    rows = dot(field_ref[...], table_ref[...], ((1,), (0,)))
    rows_to_blocks(rows, half, slab, by_rows, by_peer)

    @pl.when(half == 1)
    def _():
        out_ref[...] = by_peer[...].astype(out_ref.dtype)


def analysis(field, table):
    total, cells = field.shape
    peers = table.shape[1]
    slab = total // (2 * LANES)
    return pl.pallas_call(
        functools.partial(analysis_kernel, slab),
        out_shape=jax.ShapeDtypeStruct((peers * 2 * slab, LANES), jnp.bfloat16),
        grid=(2,),
        in_specs=[
            pl.BlockSpec((total // 2, cells), lambda h: (h, 0)),
            pl.BlockSpec(table.shape, lambda h: (0, 0)),
        ],
        out_specs=pl.BlockSpec((peers * 2 * slab, LANES), lambda h: (0, 0)),
        scratch_shapes=[
            pltpu.VMEM((total // 2, peers), jnp.float32),
            pltpu.VMEM((peers * 2 * slab, LANES), jnp.float32),
        ],
        compiler_params=params(),
        cost_estimate=pl.CostEstimate(flops=2 * total * cells * peers, bytes_accessed=3 << 20, transcendentals=0),
        name="analysis",
    )(field, table)


def mixing_matrix(spread_ref, weight_ref, slab, axis):
    spread = spread_ref[...]
    wide = dot(spread, weight_ref[...], ((1,), (axis,))).astype(jnp.bfloat16)
    full = dot(wide, spread, ((1,), (1,)))
    row = lax.broadcasted_iota(jnp.int32, full.shape, 0) % slab
    col = lax.broadcasted_iota(jnp.int32, full.shape, 1) % slab
    return jnp.where(row == col, full, 0.0).astype(jnp.bfloat16)


def pointwise_kernel(slab, axis, field_ref, weight_ref, spread_ref, bias_ref, out_ref, matrix):
    @pl.when(pl.program_id(0) == 0)
    def _():
        matrix[...] = mixing_matrix(spread_ref, weight_ref, slab, axis)

    out_ref[...] = dot(matrix[...], field_ref[...], ((1,), (0,))) + bias_ref[...]


def pointwise(field, weight, bias, axis):
    total, cells = field.shape
    channels = weight.shape[0]
    planes = 2 * LANES // channels
    rows = total // planes
    slab = rows // channels
    spread = jnp.asarray(np.kron(np.eye(channels), np.ones((slab, 1))).astype(jnp.bfloat16))
    return pl.pallas_call(
        functools.partial(pointwise_kernel, slab, axis),
        out_shape=jax.ShapeDtypeStruct((total, cells), jnp.float32),
        grid=(planes,),
        in_specs=[
            pl.BlockSpec((rows, cells), lambda z: (z, 0)),
            pl.BlockSpec(weight.shape, lambda z: (0, 0)),
            pl.BlockSpec(spread.shape, lambda z: (0, 0)),
            pl.BlockSpec((rows, 1), lambda z: (0, 0)),
        ],
        out_specs=pl.BlockSpec((rows, cells), lambda z: (z, 0)),
        scratch_shapes=[pltpu.VMEM((rows, rows), jnp.bfloat16)],
        compiler_params=params(),
        cost_estimate=pl.CostEstimate(flops=2 * total * rows * cells, bytes_accessed=6 << 20, transcendentals=0),
        name="pointwise",
    )(field, weight, spread, bias)


def owner_kernel(forward, slab, blocks_ref, into_ref, back_ref, weight_ref, out_ref, modes_ref, kept, mixed, partial):
    peers = blocks_ref.shape[0] // (2 * slab)
    channels = weight_ref.shape[0]
    planes = 2 * LANES // channels
    received = blocks_ref[...].astype(jnp.float32).reshape(peers, 2 * slab, LANES)
    for half in range(2):
        part = received[:, half * slab : (half + 1) * slab, :].reshape(peers * slab, LANES).astype(jnp.bfloat16)
        modes = dot(into_ref[...], part, ((1,), (0,))).T
        kept[half * LANES : (half + 1) * LANES, :] = modes.astype(jnp.bfloat16).astype(jnp.float32)
    modes_ref[...] = kept[...].astype(jnp.bfloat16)
    if forward:

        def step(i, sums):
            weight = weight_ref[i].astype(jnp.float32)
            return tuple(sums[z] + kept[pl.ds(z * channels + i, 1), :] * weight for z in range(planes))

        zeros = jnp.zeros((channels, LANES), jnp.float32)
        sums = lax.fori_loop(0, channels, step, (zeros,) * planes, unroll=4)
        for z in range(planes):
            mixed[z * channels : (z + 1) * channels, :] = sums[z]
    else:

        def step(i, carry):
            weight = weight_ref[i].astype(jnp.float32)
            for z in range(planes):
                product = weight * kept[z * channels : (z + 1) * channels, :]
                folded = product.reshape(channels // 8, 8, LANES).sum(axis=0)
                partial[pl.ds(pl.multiple_of((z * channels + i) * 8, 8), 8), :] = folded
            return carry

        lax.fori_loop(0, channels, step, 0, unroll=4)
        total = partial[pl.ds(0, planes * channels, stride=8), :]
        for row in range(1, 8):
            total = total + partial[pl.ds(row, planes * channels, stride=8), :]
        mixed[...] = total
    halves = []
    for half in range(2):
        part = mixed[half * LANES : (half + 1) * LANES, :].astype(jnp.bfloat16)
        spatial = dot(back_ref[...], part, ((1,), (1,)))
        halves.append(spatial.reshape(peers, slab, LANES))
    out_ref[...] = jnp.concatenate(halves, axis=1).reshape(out_ref.shape).astype(out_ref.dtype)


def owner(blocks, into, back, weight, forward):
    cells, modes = back.shape
    rows = blocks.shape[0]
    channels = weight.shape[0]
    slab = rows // (2 * LANES)
    every = pl.BlockSpec(memory_space=pltpu.VMEM)
    return pl.pallas_call(
        functools.partial(owner_kernel, forward, slab),
        out_shape=(
            jax.ShapeDtypeStruct(blocks.shape, jnp.bfloat16),
            jax.ShapeDtypeStruct((2 * LANES, modes), jnp.bfloat16),
        ),
        in_specs=[every] * 4,
        out_specs=(every, every),
        scratch_shapes=[
            pltpu.VMEM((2 * LANES, modes), jnp.float32),
            pltpu.VMEM((2 * LANES, modes), jnp.float32),
            pltpu.VMEM((8 * 2 * LANES if not forward else 8, modes), jnp.float32),
        ],
        compiler_params=params(),
        cost_estimate=pl.CostEstimate(flops=4 * rows * LANES * modes, bytes_accessed=4 << 20, transcendentals=0),
        name="owner_forward" if forward else "owner_backward",
    )(blocks, into, back, weight)


def slab_kernel(slab, step_rows, chunk, blocks_ref, local_ref, cotangent_ref, synth_ref, table_ref,
                out_ref, grad_ref, send_ref, by_peer, by_rows, pre, half_rows):
    step = pl.program_id(0)
    steps = pl.num_programs(0)

    @pl.when(step == 0)
    def _():
        blocks_to_rows(blocks_ref, slab, by_peer, by_rows)

    start = pl.multiple_of(step * step_rows, step_rows)
    modal = by_rows[pl.ds(start, step_rows), :].astype(jnp.bfloat16)
    pre[...] = dot(modal, synth_ref[...], ((1,), (0,))) + local_ref[...]

    def body(index, carry):
        here = pl.ds(pl.multiple_of(index * chunk, chunk), chunk)
        value = pre[here, :]
        size = jnp.abs(value)
        short = 1.0 / (size * TAIL_SHIFT + 1.0)
        bell = jnp.exp2(value * value * -HALF_LOG2E)
        series = short * TAIL[7] + TAIL[6]
        for coefficient in TAIL[5::-1]:
            series = series * short + coefficient
        tail = series * short * bell
        share = jnp.where(value < 0.0, tail, 1.0 - tail)
        out_ref[here, :] = (value * share).astype(out_ref.dtype)
        slope = share + value * bell * DENSITY
        grad_ref[here, :] = (cotangent_ref[here, :].astype(jnp.float32) * slope).astype(grad_ref.dtype)
        return carry

    lax.fori_loop(0, step_rows // chunk, body, 0, unroll=2)
    half_rows[pl.ds(start, step_rows), :] = dot(grad_ref[...], table_ref[...], ((1,), (0,)))

    @pl.when(step == steps - 1)
    def _():
        tiles = 2 * slab
        for half in range(2):
            for x in range(slab):
                part = half_rows[pl.ds(half * LANES * slab + x, LANES, stride=slab), :]
                by_peer[pl.ds(half * slab + x, LANES, stride=tiles), :] = part.T
        send_ref[...] = by_peer[...].astype(send_ref.dtype)


def slab_stage(blocks, local, cotangent, synth, table):
    total, cells = cotangent.shape
    modes = table.shape[1]
    slab = total // (2 * LANES)
    step_rows = 256
    moving = pl.BlockSpec((step_rows, cells), lambda s: (s, 0))

    def fixed(array):
        return pl.BlockSpec(array.shape, lambda s: (0, 0))

    return pl.pallas_call(
        functools.partial(slab_kernel, slab, step_rows, 16),
        out_shape=(
            jax.ShapeDtypeStruct((total, cells), jnp.bfloat16),
            jax.ShapeDtypeStruct((total, cells), jnp.bfloat16),
            jax.ShapeDtypeStruct(blocks.shape, jnp.bfloat16),
        ),
        grid=(total // step_rows,),
        in_specs=[fixed(blocks), moving, moving, fixed(synth), fixed(table)],
        out_specs=(moving, moving, fixed(blocks)),
        scratch_shapes=[
            pltpu.VMEM((total, modes), jnp.float32),
            pltpu.VMEM((total, modes), jnp.float32),
            pltpu.VMEM((step_rows, cells), jnp.float32),
            pltpu.VMEM((total, modes), jnp.float32),
        ],
        compiler_params=params(),
        cost_estimate=pl.CostEstimate(flops=4 * total * cells * modes, bytes_accessed=11 << 20, transcendentals=2 * total * cells),
        name="slab_stage",
    )(blocks, local, cotangent, synth, table)


def final_kernel(slab, step_rows, blocks_ref, through_ref, synth_ref, out_ref, by_peer, by_rows):
    step = pl.program_id(0)

    @pl.when(step == 0)
    def _():
        blocks_to_rows(blocks_ref, slab, by_peer, by_rows)

    start = pl.multiple_of(step * step_rows, step_rows)
    modal = by_rows[pl.ds(start, step_rows), :].astype(jnp.bfloat16)
    out_ref[...] = (dot(modal, synth_ref[...], ((1,), (0,))) + through_ref[...]).astype(out_ref.dtype)


def final_stage(blocks, through, synth):
    total, cells = through.shape
    modes = synth.shape[0]
    slab = total // (2 * LANES)
    step_rows = 512
    moving = pl.BlockSpec((step_rows, cells), lambda s: (s, 0))

    def fixed(array):
        return pl.BlockSpec(array.shape, lambda s: (0, 0))

    return pl.pallas_call(
        functools.partial(final_kernel, slab, step_rows),
        out_shape=jax.ShapeDtypeStruct((total, cells), jnp.bfloat16),
        grid=(total // step_rows,),
        in_specs=[fixed(blocks), moving, fixed(synth)],
        out_specs=moving,
        scratch_shapes=[
            pltpu.VMEM((total, modes), jnp.float32),
            pltpu.VMEM((total, modes), jnp.float32),
        ],
        compiler_params=params(),
        cost_estimate=pl.CostEstimate(flops=2 * total * cells * modes, bytes_accessed=7 << 20, transcendentals=0),
        name="final_stage",
    )(blocks, through, synth)


def weight_grad_kernel(step_channels, coeffs_ref, grads_ref, out_ref):
    channels = out_ref.shape[1]
    planes = coeffs_ref.shape[0] // channels
    first = pl.program_id(0) * step_channels

    def step(i, carry):
        total = None
        for z in range(planes):
            row = coeffs_ref[pl.ds(z * channels + first + i, 1), :]
            term = row * grads_ref[z * channels : (z + 1) * channels, :]
            total = term if total is None else total + term
        out_ref[i] = total
        return carry

    lax.fori_loop(0, step_channels, step, 0, unroll=4)


def weight_grad(coeffs, grads, channels):
    modes = coeffs.shape[1]
    step_channels = 16
    fixed = pl.BlockSpec(coeffs.shape, lambda s: (0, 0))
    return pl.pallas_call(
        functools.partial(weight_grad_kernel, step_channels),
        out_shape=jax.ShapeDtypeStruct((channels, channels, modes), jnp.float32),
        grid=(channels // step_channels,),
        in_specs=[fixed, fixed],
        out_specs=pl.BlockSpec((step_channels, channels, modes), lambda s: (s, 0, 0)),
        compiler_params=params(),
        cost_estimate=pl.CostEstimate(flops=2 * coeffs.size * channels, bytes_accessed=5 << 20, transcendentals=0),
        name="weight_grad",
    )(coeffs, grads)


def exchange(blocks, devices):
    tiles = blocks.reshape(devices, blocks.shape[0] // devices, LANES)
    return lax.all_to_all(tiles, AXES, split_axis=0, concat_axis=0, tiled=True).reshape(blocks.shape)


def shards(flow_field, cotangent, spectral_weight, local_weight, channel_bias):
    devices = lax.axis_size("gx") * lax.axis_size("gy")
    planes, channels, slab, cells_along = flow_field.shape
    cells_across = slab * devices
    kept = spectral_weight.shape[3] // 2
    forward_x = basis_table(cells_across, kept, math.sqrt(2.0 / cells_across))
    forward_y = basis_table(cells_along, kept, math.sqrt(2.0 / cells_along))
    inverse_x = basis_table(cells_across, kept, math.sqrt(1.0 / kept))
    inverse_y = basis_table(cells_along, kept, math.sqrt(1.0 / kept))

    def flip(table):
        return jnp.asarray(np.ascontiguousarray(table.T))

    field = flow_field.reshape(planes * channels * slab, cells_along)
    gradient = cotangent.reshape(field.shape)
    weight = spectral_weight.reshape(spectral_weight.shape[1:])
    bias = jnp.repeat(channel_bias, slab)[:, None]

    received = exchange(analysis(field, jnp.asarray(forward_y)), devices)
    local = pointwise(field, local_weight, bias, 1)
    modal, coeffs = owner(received, flip(forward_x), jnp.asarray(inverse_x), weight, True)
    gathered = exchange(modal, devices)
    output, grad_pre, grad_rows = slab_stage(gathered, local, gradient, flip(inverse_y), jnp.asarray(inverse_y))
    received = exchange(grad_rows, devices)
    through = pointwise(grad_pre, local_weight, jnp.zeros_like(bias), 0)
    partial, grads = owner(received, flip(inverse_x), jnp.asarray(forward_x), weight, False)
    gathered = exchange(partial, devices)
    grad_weight = weight_grad(coeffs.astype(jnp.float32), grads.astype(jnp.float32), channels)
    grad_field = final_stage(gathered, through, flip(forward_y))
    return (
        output.reshape(flow_field.shape),
        grad_field.reshape(flow_field.shape),
        grad_weight.reshape(spectral_weight.shape),
    )


def solution(mesh):
    placed = (
        P(None, None, AXES, None),
        P(None, None, AXES, None),
        P(AXES, None, None, None),
        P(),
        P(),
    )
    return jax.shard_map(
        shards,
        mesh=mesh,
        in_specs=placed,
        out_specs=(P(None, None, AXES, None), P(None, None, AXES, None), P(AXES, None, None, None)),
        check_vma=False,
    )
```

```python
import functools
import math

import jax
import jax.numpy as jnp
import numpy as np
from jax import lax
from jax.experimental import pallas as pl
from jax.experimental.pallas import tpu as pltpu
from jax.sharding import PartitionSpec as P

AXES = ("gx", "gy")
LANES = 128
VMEM_LIMIT = 20 * 1024 * 1024

ROOT_HALF = 0.7071067811865476
HALF_LOG2E = 0.5 * math.log2(math.e)
DENSITY = 0.3989422804014327


def basis_table(cells, kept, factor):
    positions = np.arange(cells, dtype=np.int64)
    columns = np.arange(2 * kept, dtype=np.int64)
    frequency = np.where(columns < kept, columns, columns - kept + 1)
    phases = positions[:, None] * frequency[None, :] % cells
    angles = phases.astype(np.float32) * np.float32(2.0 * math.pi / cells)
    values = np.where(columns[None, :] < kept, np.cos(angles), np.sin(angles))
    return (values * np.float32(factor)).astype(jnp.bfloat16)


def dot(a, b, contract):
    return lax.dot_general(a, b, (contract, ((), ())), preferred_element_type=jnp.float32)


def in_hbm(array):
    return pltpu.with_memory_space_constraint(array, pltpu.MemorySpace.HBM)


def params():
    return pltpu.CompilerParams(vmem_limit_bytes=VMEM_LIMIT)


def rows_to_blocks(half, slab, by_rows, by_peer):
    tiles = 2 * slab
    for x in range(slab):
        part = by_rows[pl.ds(half * LANES * slab + x, LANES, stride=slab), :]
        by_peer[pl.ds(half * slab + x, LANES, stride=tiles), :] = part.T


def blocks_to_rows(blocks_ref, slab, by_peer, by_rows):
    tiles = 2 * slab
    by_peer[...] = blocks_ref[...].astype(jnp.float32)
    for half in range(2):
        for x in range(slab):
            part = by_peer[pl.ds(half * slab + x, LANES, stride=tiles), :]
            by_rows[pl.ds(half * LANES * slab + x, LANES, stride=slab), :] = part.T


def fetch(pairs, sems):
    copies = [pltpu.make_async_copy(source, target, sems.at[i]) for i, (source, target) in enumerate(pairs)]
    for copy in copies:
        copy.start()
    return copies


def part_of(ref, index, parts):
    rows = ref.shape[0] // parts
    return ref.at[pl.ds(pl.multiple_of(index * rows, rows), rows), :]


def analysis_kernel(slab, parts, field_hbm, table_hbm, out_ref, by_rows, by_peer, field, table, sems):
    pairs = [(table_hbm, table)] + [(part_of(field_hbm, i, parts), part_of(field, i, parts)) for i in range(parts)]
    copies = fetch(pairs, sems)
    copies[0].wait()
    for i in range(parts):
        copies[1 + i].wait()
        part_of(by_rows, i, parts)[...] = dot(part_of(field, i, parts)[...], table[...], ((1,), (0,)))
        if 2 * (i + 1) == parts:
            rows_to_blocks(0, slab, by_rows, by_peer)
    rows_to_blocks(1, slab, by_rows, by_peer)
    out_ref[...] = by_peer[...].astype(out_ref.dtype)


EVERY = pl.BlockSpec(memory_space=pltpu.VMEM)
ANYWHERE = pl.BlockSpec(memory_space=pl.ANY)


def analysis(field, table):
    total, cells = field.shape
    peers = table.shape[1]
    slab = total // (2 * LANES)
    parts = 4
    return pl.pallas_call(
        functools.partial(analysis_kernel, slab, parts),
        out_shape=jax.ShapeDtypeStruct((peers * 2 * slab, LANES), jnp.bfloat16),
        in_specs=[ANYWHERE, ANYWHERE],
        out_specs=EVERY,
        scratch_shapes=[
            pltpu.VMEM((total, peers), jnp.float32),
            pltpu.VMEM((peers * 2 * slab, LANES), jnp.float32),
            pltpu.VMEM(field.shape, field.dtype),
            pltpu.VMEM(table.shape, table.dtype),
            pltpu.SemaphoreType.DMA((1 + parts,)),
        ],
        compiler_params=params(),
        cost_estimate=pl.CostEstimate(flops=2 * total * cells * peers, bytes_accessed=3 << 20, transcendentals=0),
        name="analysis",
    )(in_hbm(field), in_hbm(table))


def mixing_matrix(spread_ref, weight_ref, slab, axis):
    spread = spread_ref[...]
    wide = dot(spread, weight_ref[...], ((1,), (axis,))).astype(jnp.bfloat16)
    full = dot(wide, spread, ((1,), (1,)))
    row = lax.broadcasted_iota(jnp.int32, full.shape, 0) % slab
    col = lax.broadcasted_iota(jnp.int32, full.shape, 1) % slab
    return jnp.where(row == col, full, 0.0).astype(jnp.bfloat16)


def pointwise_kernel(slab, planes, field_hbm, weight_ref, spread_ref, out_hbm, field, out, matrix, sems, out_sems):
    copies = fetch([(part_of(field_hbm, z, planes), part_of(field, z, planes)) for z in range(planes)], sems)
    matrix[...] = mixing_matrix(spread_ref, weight_ref, slab, 0)
    sends = [pltpu.make_async_copy(part_of(out, z, planes), part_of(out_hbm, z, planes), out_sems.at[z]) for z in range(planes)]
    for z in range(planes):
        copies[z].wait()
        part_of(out, z, planes)[...] = dot(matrix[...], part_of(field, z, planes)[...], ((1,), (0,)))
        sends[z].start()
    for send in sends:
        send.wait()


def pointwise(field, weight):
    total, cells = field.shape
    channels = weight.shape[0]
    planes = 2 * LANES // channels
    rows = total // planes
    slab = rows // channels
    return pl.pallas_call(
        functools.partial(pointwise_kernel, slab, planes),
        out_shape=pltpu.MemorySpace.HBM((total, cells), jnp.float32),
        in_specs=[ANYWHERE, EVERY, EVERY],
        out_specs=ANYWHERE,
        scratch_shapes=[
            pltpu.VMEM(field.shape, field.dtype),
            pltpu.VMEM(field.shape, jnp.float32),
            pltpu.VMEM((rows, rows), jnp.bfloat16),
            pltpu.SemaphoreType.DMA((planes,)),
            pltpu.SemaphoreType.DMA((planes,)),
        ],
        compiler_params=params(),
        cost_estimate=pl.CostEstimate(flops=2 * total * rows * cells, bytes_accessed=6 << 20, transcendentals=0),
        name="pointwise",
    )(in_hbm(field), weight, spread_table(channels, slab))


def owner_kernel(forward, slab, blocks_ref, into_ref, back_ref, weight_ref, out_ref, modes_ref, kept, mixed, partial):
    peers = blocks_ref.shape[0] // (2 * slab)
    channels = weight_ref.shape[0]
    planes = 2 * LANES // channels
    received = blocks_ref[...].astype(jnp.float32).reshape(peers, 2 * slab, LANES)
    for half in range(2):
        part = received[:, half * slab : (half + 1) * slab, :].reshape(peers * slab, LANES).astype(jnp.bfloat16)
        modes = dot(into_ref[...], part, ((1,), (0,))).T
        kept[half * LANES : (half + 1) * LANES, :] = modes.astype(jnp.bfloat16).astype(jnp.float32)
    modes_ref[...] = kept[...].astype(jnp.bfloat16)
    if forward:

        def step(i, sums):
            weight = weight_ref[i].astype(jnp.float32)
            return tuple(sums[z] + kept[pl.ds(z * channels + i, 1), :] * weight for z in range(planes))

        zeros = jnp.zeros((channels, LANES), jnp.float32)
        sums = lax.fori_loop(0, channels, step, (zeros,) * planes, unroll=4)
        for z in range(planes):
            mixed[z * channels : (z + 1) * channels, :] = sums[z]
    else:

        def step(i, carry):
            weight = weight_ref[i].astype(jnp.float32)
            for z in range(planes):
                product = weight * kept[z * channels : (z + 1) * channels, :]
                folded = product.reshape(channels // 8, 8, LANES).sum(axis=0)
                partial[pl.ds(pl.multiple_of((z * channels + i) * 8, 8), 8), :] = folded
            return carry

        lax.fori_loop(0, channels, step, 0, unroll=4)
        total = partial[pl.ds(0, planes * channels, stride=8), :]
        for row in range(1, 8):
            total = total + partial[pl.ds(row, planes * channels, stride=8), :]
        mixed[...] = total
    halves = []
    for half in range(2):
        part = mixed[half * LANES : (half + 1) * LANES, :].astype(jnp.bfloat16)
        spatial = dot(back_ref[...], part, ((1,), (1,)))
        halves.append(spatial.reshape(peers, slab, LANES))
    out_ref[...] = jnp.concatenate(halves, axis=1).reshape(out_ref.shape).astype(out_ref.dtype)


def owner(blocks, into, back, weight, forward):
    cells, modes = back.shape
    rows = blocks.shape[0]
    channels = weight.shape[0]
    slab = rows // (2 * LANES)
    return pl.pallas_call(
        functools.partial(owner_kernel, forward, slab),
        out_shape=(
            jax.ShapeDtypeStruct(blocks.shape, jnp.bfloat16),
            jax.ShapeDtypeStruct((2 * LANES, modes), jnp.bfloat16),
        ),
        in_specs=[EVERY] * 4,
        out_specs=(EVERY, EVERY),
        scratch_shapes=[
            pltpu.VMEM((2 * LANES, modes), jnp.float32),
            pltpu.VMEM((2 * LANES, modes), jnp.float32),
            pltpu.VMEM((8 * 2 * LANES if not forward else 8, modes), jnp.float32),
        ],
        compiler_params=params(),
        cost_estimate=pl.CostEstimate(flops=4 * rows * LANES * modes, bytes_accessed=4 << 20, transcendentals=0),
        name="owner_forward" if forward else "owner_backward",
    )(blocks, into, back, weight)


def slab_kernel(slab, parts, chunk, blocks_ref, field_ref, weight_ref, spread_ref, bias_ref, cotangent_hbm, synth_hbm,
                table_hbm, out_hbm, grad_hbm, send_ref, by_peer, by_rows, half_rows, pre, matrix, offset, cotangent, synth,
                table, out, grad, sems, cotangent_sems, out_sems, grad_sems):
    rows = out.shape[0] // parts
    copies = fetch([(synth_hbm, synth), (table_hbm, table)], sems)

    def cotangent_copy(i):
        return pltpu.make_async_copy(part_of(cotangent_hbm, i, parts), part_of(cotangent, i, parts), cotangent_sems.at[i])

    for i in range(parts):
        cotangent_copy(i).start()

    def out_copy(i):
        return pltpu.make_async_copy(part_of(out, i, parts), part_of(out_hbm, i, parts), out_sems.at[i])

    def grad_copy(i):
        return pltpu.make_async_copy(part_of(grad, i, parts), part_of(grad_hbm, i, parts), grad_sems.at[i])

    matrix[...] = mixing_matrix(spread_ref, weight_ref, slab, 1)
    offset[...] = jnp.sum(spread_ref[...].astype(jnp.float32) * bias_ref[...], axis=1, keepdims=True)
    blocks_to_rows(blocks_ref, slab, by_peer, by_rows)
    for copy in copies:
        copy.wait()

    def part(i, carry):
        start = pl.multiple_of(i * rows, rows)
        modal = by_rows[pl.ds(start, rows), :].astype(jnp.bfloat16)
        local = dot(matrix[...], part_of(field_ref, i, parts)[...], ((1,), (0,)))
        pre[...] = dot(modal, synth[...], ((1,), (0,))) + local + offset[...]
        cotangent_copy(i).wait()

        def body(index, carry):
            here = pl.ds(pl.multiple_of(index * chunk, chunk), chunk)
            there = pl.ds(pl.multiple_of(start + index * chunk, chunk), chunk)
            value = pre[here, :]
            share = 0.5 + 0.5 * lax.erf(value * ROOT_HALF)
            bell = jnp.exp2(value * value * -HALF_LOG2E)
            out[there, :] = (value * share).astype(out.dtype)
            slope = share + value * bell * DENSITY
            grad[there, :] = (cotangent[there, :].astype(jnp.float32) * slope).astype(grad.dtype)
            return carry

        lax.fori_loop(0, rows // chunk, body, 0, unroll=2)
        out_copy(i).start()
        grad_copy(i).start()
        half_rows[pl.ds(start, rows), :] = dot(part_of(grad, i, parts)[...], table[...], ((1,), (0,)))
        return carry

    lax.fori_loop(0, parts, part, 0)
    for half in range(2):
        rows_to_blocks(half, slab, half_rows, by_peer)
    send_ref[...] = by_peer[...].astype(send_ref.dtype)
    for i in range(parts):
        out_copy(i).wait()
        grad_copy(i).wait()


def spread_table(channels, slab):
    return jnp.asarray(np.kron(np.eye(channels), np.ones((slab, 1))).astype(jnp.bfloat16))


def slab_stage(blocks, field, cotangent, weight, bias, synth, table):
    total, cells = cotangent.shape
    modes = table.shape[1]
    slab = total // (2 * LANES)
    channels = weight.shape[0]
    parts = 2 * LANES // channels
    rows = total // parts
    whole = (total, cells)
    return pl.pallas_call(
        functools.partial(slab_kernel, slab, parts, 16),
        out_shape=(
            pltpu.MemorySpace.HBM(whole, jnp.bfloat16),
            pltpu.MemorySpace.HBM(whole, jnp.bfloat16),
            jax.ShapeDtypeStruct(blocks.shape, jnp.bfloat16),
        ),
        in_specs=[EVERY] * 5 + [ANYWHERE] * 3,
        out_specs=(ANYWHERE, ANYWHERE, EVERY),
        scratch_shapes=[
            pltpu.VMEM((total, modes), jnp.float32),
            pltpu.VMEM((total, modes), jnp.float32),
            pltpu.VMEM((total, modes), jnp.float32),
            pltpu.VMEM((rows, cells), jnp.float32),
            pltpu.VMEM((rows, rows), jnp.bfloat16),
            pltpu.VMEM((rows, 1), jnp.float32),
            pltpu.VMEM(whole, jnp.bfloat16),
            pltpu.VMEM(synth.shape, synth.dtype),
            pltpu.VMEM(table.shape, table.dtype),
            pltpu.VMEM(whole, jnp.bfloat16),
            pltpu.VMEM(whole, jnp.bfloat16),
            pltpu.SemaphoreType.DMA((2,)),
            pltpu.SemaphoreType.DMA((parts,)),
            pltpu.SemaphoreType.DMA((parts,)),
            pltpu.SemaphoreType.DMA((parts,)),
        ],
        compiler_params=params(),
        cost_estimate=pl.CostEstimate(flops=4 * total * cells * modes, bytes_accessed=11 << 20, transcendentals=2 * total * cells),
        name="slab_stage",
    )(blocks, field, weight, spread_table(channels, slab), bias, in_hbm(cotangent), in_hbm(synth), in_hbm(table))


def final_kernel(slab, parts, blocks_any, through_hbm, synth_any, out_hbm, by_peer, by_rows, blocks, through, synth, out,
                 sems, out_sems):
    pairs = [(blocks_any, blocks), (synth_any, synth)]
    pairs += [(part_of(through_hbm, i, parts), part_of(through, i, parts)) for i in range(parts)]
    copies = fetch(pairs, sems)
    copies[0].wait()
    blocks_to_rows(blocks, slab, by_peer, by_rows)
    copies[1].wait()
    sends = [pltpu.make_async_copy(part_of(out, i, parts), part_of(out_hbm, i, parts), out_sems.at[i]) for i in range(parts)]
    for i in range(parts):
        copies[2 + i].wait()
        modal = part_of(by_rows, i, parts)[...].astype(jnp.bfloat16)
        total = dot(modal, synth[...], ((1,), (0,))) + part_of(through, i, parts)[...]
        part_of(out, i, parts)[...] = total.astype(out.dtype)
        sends[i].start()
    for send in sends:
        send.wait()


def final_stage(blocks, through, synth):
    total, cells = through.shape
    modes = synth.shape[0]
    slab = total // (2 * LANES)
    parts = 4
    return pl.pallas_call(
        functools.partial(final_kernel, slab, parts),
        out_shape=pltpu.MemorySpace.HBM((total, cells), jnp.bfloat16),
        in_specs=[ANYWHERE] * 3,
        out_specs=ANYWHERE,
        scratch_shapes=[
            pltpu.VMEM((total, modes), jnp.float32),
            pltpu.VMEM((total, modes), jnp.float32),
            pltpu.VMEM(blocks.shape, blocks.dtype),
            pltpu.VMEM(through.shape, through.dtype),
            pltpu.VMEM(synth.shape, synth.dtype),
            pltpu.VMEM(through.shape, jnp.bfloat16),
            pltpu.SemaphoreType.DMA((2 + parts,)),
            pltpu.SemaphoreType.DMA((parts,)),
        ],
        compiler_params=params(),
        cost_estimate=pl.CostEstimate(flops=2 * total * cells * modes, bytes_accessed=7 << 20, transcendentals=0),
        name="final_stage",
    )(blocks, in_hbm(through), synth)


def weight_grad_kernel(step_channels, coeffs_ref, grads_ref, out_ref):
    channels = out_ref.shape[1]
    planes = coeffs_ref.shape[0] // channels
    first = pl.program_id(0) * step_channels

    def step(i, carry):
        total = None
        for z in range(planes):
            row = coeffs_ref[pl.ds(z * channels + first + i, 1), :]
            term = row * grads_ref[z * channels : (z + 1) * channels, :]
            total = term if total is None else total + term
        out_ref[i] = total
        return carry

    lax.fori_loop(0, step_channels, step, 0, unroll=4)


def weight_grad(coeffs, grads, channels):
    modes = coeffs.shape[1]
    step_channels = 16
    fixed = pl.BlockSpec(coeffs.shape, lambda s: (0, 0))
    return pl.pallas_call(
        functools.partial(weight_grad_kernel, step_channels),
        out_shape=jax.ShapeDtypeStruct((channels, channels, modes), jnp.float32),
        grid=(channels // step_channels,),
        in_specs=[fixed, fixed],
        out_specs=pl.BlockSpec((step_channels, channels, modes), lambda s: (s, 0, 0)),
        compiler_params=params(),
        cost_estimate=pl.CostEstimate(flops=2 * coeffs.size * channels, bytes_accessed=5 << 20, transcendentals=0),
        name="weight_grad",
    )(coeffs, grads)


def exchange(blocks, devices):
    tiles = blocks.reshape(devices, blocks.shape[0] // devices, LANES)
    return lax.all_to_all(tiles, AXES, split_axis=0, concat_axis=0, tiled=True).reshape(blocks.shape)


def shards(flow_field, cotangent, spectral_weight, local_weight, channel_bias):
    devices = lax.axis_size("gx") * lax.axis_size("gy")
    planes, channels, slab, cells_along = flow_field.shape
    cells_across = slab * devices
    kept = spectral_weight.shape[3] // 2
    forward_x = basis_table(cells_across, kept, math.sqrt(2.0 / cells_across))
    forward_y = basis_table(cells_along, kept, math.sqrt(2.0 / cells_along))
    inverse_x = basis_table(cells_across, kept, math.sqrt(1.0 / kept))
    inverse_y = basis_table(cells_along, kept, math.sqrt(1.0 / kept))

    def flip(table):
        return jnp.asarray(np.ascontiguousarray(table.T))

    field = flow_field.reshape(planes * channels * slab, cells_along)
    gradient = cotangent.reshape(field.shape)
    weight = spectral_weight.reshape(spectral_weight.shape[1:])
    bias = channel_bias[None, :]

    received = exchange(analysis(field, jnp.asarray(forward_y)), devices)
    modal, coeffs = owner(received, flip(forward_x), jnp.asarray(inverse_x), weight, True)
    gathered = exchange(modal, devices)
    output, grad_pre, grad_rows = slab_stage(
        gathered, field, gradient, local_weight, bias, flip(inverse_y), jnp.asarray(inverse_y)
    )
    received = exchange(grad_rows, devices)
    through = pointwise(grad_pre, local_weight)
    partial, grads = owner(received, flip(inverse_x), jnp.asarray(forward_x), weight, False)
    gathered = exchange(partial, devices)
    grad_weight = weight_grad(coeffs.astype(jnp.float32), grads.astype(jnp.float32), channels)
    grad_field = final_stage(gathered, through, flip(forward_y))
    return (
        output.reshape(flow_field.shape),
        grad_field.reshape(flow_field.shape),
        grad_weight.reshape(spectral_weight.shape),
    )


def solution(mesh):
    placed = (
        P(None, None, AXES, None),
        P(None, None, AXES, None),
        P(AXES, None, None, None),
        P(),
        P(),
    )
    return jax.shard_map(
        shards,
        mesh=mesh,
        in_specs=placed,
        out_specs=(P(None, None, AXES, None), P(None, None, AXES, None), P(AXES, None, None, None)),
        check_vma=False,
    )
```

```python
import functools
import math

import jax
import jax.numpy as jnp
import numpy as np
from jax import lax
from jax.experimental import pallas as pl
from jax.experimental.pallas import tpu as pltpu
from jax.sharding import PartitionSpec as P

AXES = ("gx", "gy")
LANES = 128
VMEM_LIMIT = 20 * 1024 * 1024

ROOT_HALF = 0.7071067811865476
HALF_LOG2E = 0.5 * math.log2(math.e)
DENSITY = 0.3989422804014327


def basis_table(cells, kept, factor):
    positions = np.arange(cells, dtype=np.int64)
    columns = np.arange(2 * kept, dtype=np.int64)
    frequency = np.where(columns < kept, columns, columns - kept + 1)
    phases = positions[:, None] * frequency[None, :] % cells
    angles = phases.astype(np.float32) * np.float32(2.0 * math.pi / cells)
    values = np.where(columns[None, :] < kept, np.cos(angles), np.sin(angles))
    return (values * np.float32(factor)).astype(jnp.bfloat16)


def dot(a, b, contract):
    return lax.dot_general(a, b, (contract, ((), ())), preferred_element_type=jnp.float32)


def in_hbm(array):
    return pltpu.with_memory_space_constraint(array, pltpu.MemorySpace.HBM)


def params():
    return pltpu.CompilerParams(vmem_limit_bytes=VMEM_LIMIT)


def rows_to_blocks(half, slab, by_rows, by_peer):
    tiles = 2 * slab
    for x in range(slab):
        part = by_rows[pl.ds(half * LANES * slab + x, LANES, stride=slab), :]
        by_peer[pl.ds(half * slab + x, LANES, stride=tiles), :] = part.T


def blocks_to_rows(blocks_ref, slab, by_peer, by_rows):
    tiles = 2 * slab
    by_peer[...] = blocks_ref[...].astype(jnp.float32)
    for half in range(2):
        for x in range(slab):
            part = by_peer[pl.ds(half * slab + x, LANES, stride=tiles), :]
            by_rows[pl.ds(half * LANES * slab + x, LANES, stride=slab), :] = part.T


def fetch(pairs, sems):
    copies = [pltpu.make_async_copy(source, target, sems.at[i]) for i, (source, target) in enumerate(pairs)]
    for copy in copies:
        copy.start()
    return copies


def part_of(ref, index, parts):
    rows = ref.shape[0] // parts
    return ref.at[pl.ds(pl.multiple_of(index * rows, rows), rows), :]


def analysis_kernel(slab, parts, field_hbm, table_hbm, out_ref, by_rows, by_peer, field, table, sems):
    pairs = [(table_hbm, table)] + [(part_of(field_hbm, i, parts), part_of(field, i, parts)) for i in range(parts)]
    copies = fetch(pairs, sems)
    copies[0].wait()
    for i in range(parts):
        copies[1 + i].wait()
        part_of(by_rows, i, parts)[...] = dot(part_of(field, i, parts)[...], table[...], ((1,), (0,)))
        if 2 * (i + 1) == parts:
            rows_to_blocks(0, slab, by_rows, by_peer)
    rows_to_blocks(1, slab, by_rows, by_peer)
    out_ref[...] = by_peer[...].astype(out_ref.dtype)


EVERY = pl.BlockSpec(memory_space=pltpu.VMEM)
ANYWHERE = pl.BlockSpec(memory_space=pl.ANY)


def analysis(field, table):
    total, cells = field.shape
    peers = table.shape[1]
    slab = total // (2 * LANES)
    parts = 4
    return pl.pallas_call(
        functools.partial(analysis_kernel, slab, parts),
        out_shape=jax.ShapeDtypeStruct((peers * 2 * slab, LANES), jnp.bfloat16),
        in_specs=[ANYWHERE, ANYWHERE],
        out_specs=EVERY,
        scratch_shapes=[
            pltpu.VMEM((total, peers), jnp.float32),
            pltpu.VMEM((peers * 2 * slab, LANES), jnp.float32),
            pltpu.VMEM(field.shape, field.dtype),
            pltpu.VMEM(table.shape, table.dtype),
            pltpu.SemaphoreType.DMA((1 + parts,)),
        ],
        compiler_params=params(),
        cost_estimate=pl.CostEstimate(flops=2 * total * cells * peers, bytes_accessed=3 << 20, transcendentals=0),
        name="analysis",
    )(in_hbm(field), in_hbm(table))


def mixing_matrix(spread_ref, weight_ref, slab, axis):
    spread = spread_ref[...]
    wide = dot(spread, weight_ref[...], ((1,), (axis,))).astype(jnp.bfloat16)
    full = dot(wide, spread, ((1,), (1,)))
    row = lax.broadcasted_iota(jnp.int32, full.shape, 0) % slab
    col = lax.broadcasted_iota(jnp.int32, full.shape, 1) % slab
    return jnp.where(row == col, full, 0.0).astype(jnp.bfloat16)


def owner_kernel(forward, slab, blocks_ref, into_ref, back_ref, weight_ref, out_ref, modes_ref, kept, mixed, partial, out, sems):
    peers = blocks_ref.shape[0] // (2 * slab)
    channels = weight_ref.shape[0]
    planes = 2 * LANES // channels
    received = blocks_ref[...].astype(jnp.float32).reshape(peers, 2 * slab, LANES)
    for half in range(2):
        part = received[:, half * slab : (half + 1) * slab, :].reshape(peers * slab, LANES).astype(jnp.bfloat16)
        modes = dot(into_ref[...], part, ((1,), (0,))).T
        kept[half * LANES : (half + 1) * LANES, :] = modes.astype(jnp.bfloat16).astype(jnp.float32)
    modes_ref[...] = kept[...].astype(jnp.bfloat16)
    if forward:

        def step(i, sums):
            weight = weight_ref[i].astype(jnp.float32)
            return tuple(sums[z] + kept[pl.ds(z * channels + i, 1), :] * weight for z in range(planes))

        zeros = jnp.zeros((channels, LANES), jnp.float32)
        sums = lax.fori_loop(0, channels, step, (zeros,) * planes, unroll=4)
        for z in range(planes):
            mixed[z * channels : (z + 1) * channels, :] = sums[z]
    else:

        def step(i, carry):
            weight = weight_ref[i].astype(jnp.float32)
            for z in range(planes):
                product = weight * kept[z * channels : (z + 1) * channels, :]
                folded = product.reshape(channels // 8, 8, LANES).sum(axis=0)
                partial[pl.ds(pl.multiple_of((z * channels + i) * 8, 8), 8), :] = folded
            return carry

        lax.fori_loop(0, channels, step, 0, unroll=4)
        total = partial[pl.ds(0, planes * channels, stride=8), :]
        for row in range(1, 8):
            total = total + partial[pl.ds(row, planes * channels, stride=8), :]
        mixed[...] = total
    pieces = 1 if forward else 4
    group = peers // pieces
    sent = []
    for i in range(pieces):
        halves = []
        for half in range(2):
            part = mixed[half * LANES : (half + 1) * LANES, :].astype(jnp.bfloat16)
            spatial = dot(back_ref[i * group * slab : (i + 1) * group * slab, :], part, ((1,), (1,)))
            halves.append(spatial.reshape(group, slab, LANES))
        tiles = jnp.concatenate(halves, axis=1).reshape(group * 2 * slab, LANES).astype(out_ref.dtype)
        if forward:
            out_ref[...] = tiles
        else:
            part_of(out, i, pieces)[...] = tiles
            sent.append(pltpu.make_async_copy(part_of(out, i, pieces), part_of(out_ref, i, pieces), sems.at[i]))
            sent[i].start()
    for copy in sent:
        copy.wait()


def owner(blocks, into, back, weight, forward):
    cells, modes = back.shape
    rows = blocks.shape[0]
    channels = weight.shape[0]
    slab = rows // (2 * LANES)
    return pl.pallas_call(
        functools.partial(owner_kernel, forward, slab),
        out_shape=(
            (jax.ShapeDtypeStruct if forward else pltpu.MemorySpace.HBM)(blocks.shape, jnp.bfloat16),
            jax.ShapeDtypeStruct((2 * LANES, modes), jnp.bfloat16),
        ),
        in_specs=[EVERY] * 4,
        out_specs=(EVERY if forward else ANYWHERE, EVERY),
        scratch_shapes=[
            pltpu.VMEM((2 * LANES, modes), jnp.float32),
            pltpu.VMEM((2 * LANES, modes), jnp.float32),
            pltpu.VMEM((8 if forward else 8 * 2 * LANES, modes), jnp.float32),
            pltpu.VMEM((16, LANES) if forward else blocks.shape, jnp.bfloat16),
            pltpu.SemaphoreType.DMA((4,)),
        ],
        compiler_params=params(),
        cost_estimate=pl.CostEstimate(flops=4 * rows * LANES * modes, bytes_accessed=4 << 20, transcendentals=0),
        name="owner_forward" if forward else "owner_backward",
    )(blocks, into, back, weight)


def slab_kernel(slab, planes, chunk, blocks_ref, field_ref, weight_ref, spread_ref, bias_ref, cotangent_ref, synth_ref,
                table_ref, out_hbm, grad_hbm, send_ref, by_peer, by_rows, half_rows, pre_even, pre_odd, matrix, offset, out,
                grad_ref, out_sems, grad_sems):
    plane_rows = out.shape[0] // planes
    rows = plane_rows // 2

    def out_copy(z):
        return pltpu.make_async_copy(part_of(out, z, planes), part_of(out_hbm, z, planes), out_sems.at[z])

    def grad_copy(z):
        return pltpu.make_async_copy(part_of(grad_ref, z, planes), part_of(grad_hbm, z, planes), grad_sems.at[z])

    def fill(target, z, half):
        start = pl.multiple_of(z * plane_rows + half * rows, rows)
        modal = by_rows[pl.ds(start, rows), :].astype(jnp.bfloat16)
        mix = matrix[half * rows : (half + 1) * rows, :]
        local = dot(mix, part_of(field_ref, z, planes)[...], ((1,), (0,)))
        target[...] = dot(modal, synth_ref[...], ((1,), (0,))) + local + offset[half * rows : (half + 1) * rows, :]

    def activate(source, z, half):
        start = pl.multiple_of(z * plane_rows + half * rows, rows)
        for index in range(rows // chunk):
            there = pl.ds(pl.multiple_of(start + index * chunk, chunk), chunk)
            value = source[index * chunk : (index + 1) * chunk, :]
            share = 0.5 + 0.5 * lax.erf(value * ROOT_HALF)
            bell = jnp.exp2(value * value * -HALF_LOG2E)
            out[there, :] = (value * share).astype(out.dtype)
            slope = share + value * bell * DENSITY
            grad_ref[there, :] = (cotangent_ref[there, :].astype(jnp.float32) * slope).astype(grad_ref.dtype)

    def analyse(z, half):
        here = pl.ds(pl.multiple_of(z * plane_rows + half * rows, rows), rows)
        half_rows[here, :] = dot(grad_ref[here, :], table_ref[...], ((1,), (0,)))

    matrix[...] = mixing_matrix(spread_ref, weight_ref, slab, 1)
    offset[...] = jnp.sum(spread_ref[...].astype(jnp.float32) * bias_ref[...], axis=1, keepdims=True)
    blocks_to_rows(blocks_ref, slab, by_peer, by_rows)
    fill(pre_even, 0, 0)

    def plane(z, carry):
        fill(pre_odd, z, 1)
        activate(pre_even, z, 0)
        fill(pre_even, jnp.minimum(z + 1, planes - 1), 0)
        activate(pre_odd, z, 1)
        out_copy(z).start()
        grad_copy(z).start()
        analyse(z, 0)
        analyse(z, 1)
        return carry

    lax.fori_loop(0, planes, plane, 0)
    for half in range(2):
        rows_to_blocks(half, slab, half_rows, by_peer)
    send_ref[...] = by_peer[...].astype(send_ref.dtype)
    for z in range(planes):
        out_copy(z).wait()
        grad_copy(z).wait()


def spread_table(channels, slab):
    return jnp.asarray(np.kron(np.eye(channels), np.ones((slab, 1))).astype(jnp.bfloat16))


def slab_stage(blocks, field, cotangent, weight, bias, synth, table):
    total, cells = cotangent.shape
    modes = table.shape[1]
    slab = total // (2 * LANES)
    channels = weight.shape[0]
    planes = 2 * LANES // channels
    rows = total // planes
    whole = (total, cells)
    return pl.pallas_call(
        functools.partial(slab_kernel, slab, planes, 16),
        out_shape=(
            pltpu.MemorySpace.HBM(whole, jnp.bfloat16),
            pltpu.MemorySpace.HBM(whole, jnp.bfloat16),
            jax.ShapeDtypeStruct(blocks.shape, jnp.bfloat16),
        ),
        in_specs=[EVERY] * 8,
        out_specs=(ANYWHERE, ANYWHERE, EVERY),
        scratch_shapes=[
            pltpu.VMEM((total, modes), jnp.float32),
            pltpu.VMEM((total, modes), jnp.float32),
            pltpu.VMEM((total, modes), jnp.float32),
            pltpu.VMEM((rows // 2, cells), jnp.float32),
            pltpu.VMEM((rows // 2, cells), jnp.float32),
            pltpu.VMEM((rows, rows), jnp.bfloat16),
            pltpu.VMEM((rows, 1), jnp.float32),
            pltpu.VMEM(whole, jnp.bfloat16),
            pltpu.VMEM(whole, jnp.bfloat16),
            pltpu.SemaphoreType.DMA((planes,)),
            pltpu.SemaphoreType.DMA((planes,)),
        ],
        compiler_params=params(),
        cost_estimate=pl.CostEstimate(flops=4 * total * cells * modes, bytes_accessed=11 << 20, transcendentals=2 * total * cells),
        name="slab_stage",
    )(blocks, field, weight, spread_table(channels, slab), bias, cotangent, synth, table)


def pointwise_kernel(slab, planes, field_ref, weight_ref, spread_ref, out_ref, matrix):
    matrix[...] = mixing_matrix(spread_ref, weight_ref, slab, 0)
    for z in range(planes):
        product = dot(matrix[...], part_of(field_ref, z, planes)[...], ((1,), (0,)))
        part_of(out_ref, z, planes)[...] = product.astype(out_ref.dtype)


def pointwise(field, weight):
    total, cells = field.shape
    channels = weight.shape[0]
    planes = 2 * LANES // channels
    rows = total // planes
    slab = rows // channels
    return pl.pallas_call(
        functools.partial(pointwise_kernel, slab, planes),
        out_shape=jax.ShapeDtypeStruct((total, cells), jnp.bfloat16),
        in_specs=[EVERY] * 3,
        out_specs=EVERY,
        scratch_shapes=[pltpu.VMEM((rows, rows), jnp.bfloat16)],
        compiler_params=params(),
        cost_estimate=pl.CostEstimate(flops=2 * total * rows * cells, bytes_accessed=6 << 20, transcendentals=0),
        name="pointwise",
    )(field, weight, spread_table(channels, slab))


def final_kernel(slab, planes, blocks_ref, through_ref, synth_ref, out_hbm, by_peer, by_rows, out, out_sems):
    blocks_to_rows(blocks_ref, slab, by_peer, by_rows)
    sends = [pltpu.make_async_copy(part_of(out, z, planes), part_of(out_hbm, z, planes), out_sems.at[z]) for z in range(planes)]
    for z in range(planes):
        modal = part_of(by_rows, z, planes)[...].astype(jnp.bfloat16)
        through = part_of(through_ref, z, planes)[...].astype(jnp.float32)
        part_of(out, z, planes)[...] = (dot(modal, synth_ref[...], ((1,), (0,))) + through).astype(out.dtype)
        sends[z].start()
    for send in sends:
        send.wait()


def final_stage(blocks, through, synth):
    total, cells = through.shape
    modes = synth.shape[0]
    slab = total // (2 * LANES)
    planes = 4
    return pl.pallas_call(
        functools.partial(final_kernel, slab, planes),
        out_shape=pltpu.MemorySpace.HBM((total, cells), jnp.bfloat16),
        in_specs=[EVERY] * 3,
        out_specs=ANYWHERE,
        scratch_shapes=[
            pltpu.VMEM((total, modes), jnp.float32),
            pltpu.VMEM((total, modes), jnp.float32),
            pltpu.VMEM((total, cells), jnp.bfloat16),
            pltpu.SemaphoreType.DMA((planes,)),
        ],
        compiler_params=params(),
        cost_estimate=pl.CostEstimate(flops=2 * total * cells * modes, bytes_accessed=7 << 20, transcendentals=0),
        name="final_stage",
    )(blocks, through, synth)


def weight_grad_kernel(step_channels, coeffs_ref, grads_ref, out_ref):
    channels = out_ref.shape[1]
    planes = coeffs_ref.shape[0] // channels
    first = pl.program_id(0) * step_channels

    def step(i, carry):
        total = None
        for z in range(planes):
            row = coeffs_ref[pl.ds(z * channels + first + i, 1), :]
            term = row * grads_ref[z * channels : (z + 1) * channels, :]
            total = term if total is None else total + term
        out_ref[i] = total
        return carry

    lax.fori_loop(0, step_channels, step, 0, unroll=4)


def weight_grad(coeffs, grads, channels):
    modes = coeffs.shape[1]
    step_channels = 16
    fixed = pl.BlockSpec(coeffs.shape, lambda s: (0, 0))
    return pl.pallas_call(
        functools.partial(weight_grad_kernel, step_channels),
        out_shape=jax.ShapeDtypeStruct((channels, channels, modes), jnp.float32),
        grid=(channels // step_channels,),
        in_specs=[fixed, fixed],
        out_specs=pl.BlockSpec((step_channels, channels, modes), lambda s: (s, 0, 0)),
        compiler_params=params(),
        cost_estimate=pl.CostEstimate(flops=2 * coeffs.size * channels, bytes_accessed=5 << 20, transcendentals=0),
        name="weight_grad",
    )(coeffs, grads)


def exchange(blocks, devices):
    tiles = blocks.reshape(devices, blocks.shape[0] // devices, LANES)
    return lax.all_to_all(tiles, AXES, split_axis=0, concat_axis=0, tiled=True).reshape(blocks.shape)


def shards(flow_field, cotangent, spectral_weight, local_weight, channel_bias):
    devices = lax.axis_size("gx") * lax.axis_size("gy")
    planes, channels, slab, cells_along = flow_field.shape
    cells_across = slab * devices
    kept = spectral_weight.shape[3] // 2
    forward_x = basis_table(cells_across, kept, math.sqrt(2.0 / cells_across))
    forward_y = basis_table(cells_along, kept, math.sqrt(2.0 / cells_along))
    inverse_x = basis_table(cells_across, kept, math.sqrt(1.0 / kept))
    inverse_y = basis_table(cells_along, kept, math.sqrt(1.0 / kept))

    def flip(table):
        return jnp.asarray(np.ascontiguousarray(table.T))

    field = flow_field.reshape(planes * channels * slab, cells_along)
    gradient = cotangent.reshape(field.shape)
    weight = spectral_weight.reshape(spectral_weight.shape[1:])
    bias = channel_bias[None, :]

    received = exchange(analysis(field, jnp.asarray(forward_y)), devices)
    modal, coeffs = owner(received, flip(forward_x), jnp.asarray(inverse_x), weight, True)
    gathered = exchange(modal, devices)
    output, grad_pre, grad_rows = slab_stage(
        gathered, field, gradient, local_weight, bias, flip(inverse_y), jnp.asarray(inverse_y)
    )
    received = exchange(grad_rows, devices)
    partial, grads = owner(received, flip(inverse_x), jnp.asarray(forward_x), weight, False)
    gathered = exchange(partial, devices)
    grad_weight = weight_grad(coeffs.astype(jnp.float32), grads.astype(jnp.float32), channels)
    grad_field = final_stage(gathered, pointwise(grad_pre, local_weight), flip(forward_y))
    return (
        output.reshape(flow_field.shape),
        grad_field.reshape(flow_field.shape),
        grad_weight.reshape(spectral_weight.shape),
    )


def solution(mesh):
    placed = (
        P(None, None, AXES, None),
        P(None, None, AXES, None),
        P(AXES, None, None, None),
        P(),
        P(),
    )
    return jax.shard_map(
        shards,
        mesh=mesh,
        in_specs=placed,
        out_specs=(P(None, None, AXES, None), P(None, None, AXES, None), P(AXES, None, None, None)),
        check_vma=False,
    )
```

```python
import functools
import math

import jax
import jax.numpy as jnp
import numpy as np
from jax import lax
from jax.experimental import pallas as pl
from jax.experimental.pallas import tpu as pltpu
from jax.sharding import PartitionSpec as P

AXES = ("gx", "gy")
LANES = 128
VMEM_LIMIT = 20 * 1024 * 1024

ROOT_HALF = 0.7071067811865476
HALF_LOG2E = 0.5 * math.log2(math.e)
DENSITY = 0.3989422804014327


def basis_table(cells, kept, factor):
    positions = np.arange(cells, dtype=np.int64)
    columns = np.arange(2 * kept, dtype=np.int64)
    frequency = np.where(columns < kept, columns, columns - kept + 1)
    phases = positions[:, None] * frequency[None, :] % cells
    angles = phases.astype(np.float32) * np.float32(2.0 * math.pi / cells)
    values = np.where(columns[None, :] < kept, np.cos(angles), np.sin(angles))
    return (values * np.float32(factor)).astype(jnp.bfloat16)


def dot(a, b, contract):
    return lax.dot_general(a, b, (contract, ((), ())), preferred_element_type=jnp.float32)


def in_hbm(array):
    return pltpu.with_memory_space_constraint(array, pltpu.MemorySpace.HBM)


def params():
    return pltpu.CompilerParams(vmem_limit_bytes=VMEM_LIMIT)


def rows_to_blocks(half, slab, by_rows, by_peer):
    tiles = 2 * slab
    for x in range(slab):
        part = by_rows[pl.ds(half * LANES * slab + x, LANES, stride=slab), :]
        by_peer[pl.ds(half * slab + x, LANES, stride=tiles), :] = part.T


def blocks_to_rows(blocks_ref, slab, by_peer, by_rows):
    tiles = 2 * slab
    by_peer[...] = blocks_ref[...].astype(jnp.float32)
    for half in range(2):
        for x in range(slab):
            part = by_peer[pl.ds(half * slab + x, LANES, stride=tiles), :]
            by_rows[pl.ds(half * LANES * slab + x, LANES, stride=slab), :] = part.T


def fetch(pairs, sems):
    copies = [pltpu.make_async_copy(source, target, sems.at[i]) for i, (source, target) in enumerate(pairs)]
    for copy in copies:
        copy.start()
    return copies


def part_of(ref, index, parts):
    rows = ref.shape[0] // parts
    return ref.at[pl.ds(pl.multiple_of(index * rows, rows), rows), :]


def analysis_kernel(slab, pieces, field_hbm, table_hbm, out_ref, by_rows, by_peer, field, table, sems):
    pairs = [(table_hbm, table)]
    pairs += [(part_of(field_hbm, i, 2 * pieces), part_of(field, i, 2 * pieces)) for i in range(pieces)]
    pairs += [(part_of(field_hbm, 1, 2), part_of(field, 1, 2))]
    copies = fetch(pairs, sems)
    for half in range(2):
        for copy in copies[-1:] if half else copies[:-1]:
            copy.wait()
        part_of(by_rows, half, 2)[...] = dot(part_of(field, half, 2)[...], table[...], ((1,), (0,)))
        rows_to_blocks(half, slab, by_rows, by_peer)
    out_ref[...] = by_peer[...].astype(out_ref.dtype)


EVERY = pl.BlockSpec(memory_space=pltpu.VMEM)
ANYWHERE = pl.BlockSpec(memory_space=pl.ANY)


def analysis(field, table):
    total, cells = field.shape
    peers = table.shape[1]
    slab = total // (2 * LANES)
    pieces = 4
    return pl.pallas_call(
        functools.partial(analysis_kernel, slab, pieces),
        out_shape=jax.ShapeDtypeStruct((peers * 2 * slab, LANES), jnp.bfloat16),
        in_specs=[ANYWHERE, ANYWHERE],
        out_specs=EVERY,
        scratch_shapes=[
            pltpu.VMEM((total, peers), jnp.float32),
            pltpu.VMEM((peers * 2 * slab, LANES), jnp.float32),
            pltpu.VMEM(field.shape, field.dtype),
            pltpu.VMEM(table.shape, table.dtype),
            pltpu.SemaphoreType.DMA((2 + pieces,)),
        ],
        compiler_params=params(),
        cost_estimate=pl.CostEstimate(flops=2 * total * cells * peers, bytes_accessed=3 << 20, transcendentals=0),
        name="analysis",
    )(in_hbm(field), in_hbm(table))


def mixing_matrix(spread_ref, weight_ref, slab, axis):
    spread = spread_ref[...]
    wide = dot(spread, weight_ref[...], ((1,), (axis,))).astype(jnp.bfloat16)
    full = dot(wide, spread, ((1,), (1,)))
    row = lax.broadcasted_iota(jnp.int32, full.shape, 0) % slab
    col = lax.broadcasted_iota(jnp.int32, full.shape, 1) % slab
    return jnp.where(row == col, full, 0.0).astype(jnp.bfloat16)


def owner_kernel(forward, slab, blocks_ref, into_ref, back_ref, weight_ref, out_ref, modes_ref, kept, mixed, partial, out, sems):
    peers = blocks_ref.shape[0] // (2 * slab)
    channels = weight_ref.shape[0]
    planes = 2 * LANES // channels
    received = blocks_ref[...].astype(jnp.float32).reshape(peers, 2 * slab, LANES)
    for half in range(2):
        part = received[:, half * slab : (half + 1) * slab, :].reshape(peers * slab, LANES).astype(jnp.bfloat16)
        modes = dot(into_ref[...], part, ((1,), (0,))).T
        kept[half * LANES : (half + 1) * LANES, :] = modes.astype(jnp.bfloat16).astype(jnp.float32)
    modes_ref[...] = kept[...].astype(jnp.bfloat16)
    if forward:

        def step(i, sums):
            weight = weight_ref[i].astype(jnp.float32)
            return tuple(sums[z] + kept[pl.ds(z * channels + i, 1), :] * weight for z in range(planes))

        zeros = jnp.zeros((channels, LANES), jnp.float32)
        sums = lax.fori_loop(0, channels, step, (zeros,) * planes, unroll=4)
        for z in range(planes):
            mixed[z * channels : (z + 1) * channels, :] = sums[z]
    else:

        def step(i, carry):
            weight = weight_ref[i].astype(jnp.float32)
            for z in range(planes):
                product = weight * kept[z * channels : (z + 1) * channels, :]
                folded = product.reshape(channels // 8, 8, LANES).sum(axis=0)
                partial[pl.ds(pl.multiple_of((z * channels + i) * 8, 8), 8), :] = folded
            return carry

        lax.fori_loop(0, channels, step, 0, unroll=4)
        total = partial[pl.ds(0, planes * channels, stride=8), :]
        for row in range(1, 8):
            total = total + partial[pl.ds(row, planes * channels, stride=8), :]
        mixed[...] = total
    pieces = 1 if forward else 4
    group = peers // pieces
    sent = []
    for i in range(pieces):
        halves = []
        for half in range(2):
            part = mixed[half * LANES : (half + 1) * LANES, :].astype(jnp.bfloat16)
            spatial = dot(back_ref[i * group * slab : (i + 1) * group * slab, :], part, ((1,), (1,)))
            halves.append(spatial.reshape(group, slab, LANES))
        tiles = jnp.concatenate(halves, axis=1).reshape(group * 2 * slab, LANES).astype(out_ref.dtype)
        if forward:
            out_ref[...] = tiles
        else:
            part_of(out, i, pieces)[...] = tiles
            sent.append(pltpu.make_async_copy(part_of(out, i, pieces), part_of(out_ref, i, pieces), sems.at[i]))
            sent[i].start()
    for copy in sent:
        copy.wait()


def owner(blocks, into, back, weight, forward):
    cells, modes = back.shape
    rows = blocks.shape[0]
    channels = weight.shape[0]
    slab = rows // (2 * LANES)
    return pl.pallas_call(
        functools.partial(owner_kernel, forward, slab),
        out_shape=(
            (jax.ShapeDtypeStruct if forward else pltpu.MemorySpace.HBM)(blocks.shape, jnp.bfloat16),
            jax.ShapeDtypeStruct((2 * LANES, modes), jnp.bfloat16),
        ),
        in_specs=[EVERY] * 4,
        out_specs=(EVERY if forward else ANYWHERE, EVERY),
        scratch_shapes=[
            pltpu.VMEM((2 * LANES, modes), jnp.float32),
            pltpu.VMEM((2 * LANES, modes), jnp.float32),
            pltpu.VMEM((8 if forward else 8 * 2 * LANES, modes), jnp.float32),
            pltpu.VMEM((16, LANES) if forward else blocks.shape, jnp.bfloat16),
            pltpu.SemaphoreType.DMA((4,)),
        ],
        compiler_params=params(),
        cost_estimate=pl.CostEstimate(flops=4 * rows * LANES * modes, bytes_accessed=4 << 20, transcendentals=0),
        name="owner_forward" if forward else "owner_backward",
    )(blocks, into, back, weight)


def slab_kernel(slab, planes, chunk, blocks_ref, field_ref, weight_ref, spread_ref, bias_ref, cotangent_ref, synth_ref,
                table_ref, out_hbm, grad_hbm, send_ref, by_peer, by_rows, half_rows, pre_even, pre_odd, matrix, offset, out,
                grad_ref, out_sems, grad_sems):
    plane_rows = out.shape[0] // planes
    rows = plane_rows // 2

    def out_copy(i):
        return pltpu.make_async_copy(part_of(out, i, 2 * planes), part_of(out_hbm, i, 2 * planes), out_sems.at[i])

    def grad_copy(i):
        return pltpu.make_async_copy(part_of(grad_ref, i, 2 * planes), part_of(grad_hbm, i, 2 * planes), grad_sems.at[i])

    def fill(target, z, half):
        start = z * plane_rows + half * rows
        modal = by_rows[pl.ds(start, rows), :].astype(jnp.bfloat16)
        mix = matrix[half * rows : (half + 1) * rows, :]
        local = dot(mix, part_of(field_ref, z, planes)[...], ((1,), (0,)))
        target[...] = dot(modal, synth_ref[...], ((1,), (0,))) + local + offset[half * rows : (half + 1) * rows, :]

    def activate(source, z, half):
        start = z * plane_rows + half * rows
        for index in range(rows // chunk):
            there = pl.ds(start + index * chunk, chunk)
            value = source[index * chunk : (index + 1) * chunk, :]
            share = 0.5 + 0.5 * lax.erf(value * ROOT_HALF)
            bell = jnp.exp2(value * value * -HALF_LOG2E)
            out[there, :] = (value * share).astype(out.dtype)
            slope = share + value * bell * DENSITY
            grad_ref[there, :] = (cotangent_ref[there, :].astype(jnp.float32) * slope).astype(grad_ref.dtype)
        out_copy(2 * z + half).start()
        grad_copy(2 * z + half).start()

    def analyse(z, half):
        here = pl.ds(z * plane_rows + half * rows, rows)
        half_rows[here, :] = dot(grad_ref[here, :], table_ref[...], ((1,), (0,)))

    matrix[...] = mixing_matrix(spread_ref, weight_ref, slab, 1)
    offset[...] = jnp.sum(spread_ref[...].astype(jnp.float32) * bias_ref[...], axis=1, keepdims=True)
    blocks_to_rows(blocks_ref, slab, by_peer, by_rows)
    fill(pre_even, 0, 0)

    def plane(z):
        fill(pre_odd, z, 1)
        activate(pre_even, z, 0)
        analyse(z, 0)
        if z + 1 < planes:
            fill(pre_even, z + 1, 0)
        activate(pre_odd, z, 1)
        analyse(z, 1)

    for z in range(planes):
        plane(z)
    for half in range(2):
        rows_to_blocks(half, slab, half_rows, by_peer)
    send_ref[...] = by_peer[...].astype(send_ref.dtype)
    for i in range(2 * planes):
        out_copy(i).wait()
        grad_copy(i).wait()


def spread_table(channels, slab):
    return jnp.asarray(np.kron(np.eye(channels), np.ones((slab, 1))).astype(jnp.bfloat16))


def slab_stage(blocks, field, cotangent, weight, bias, synth, table):
    total, cells = cotangent.shape
    modes = table.shape[1]
    slab = total // (2 * LANES)
    channels = weight.shape[0]
    planes = 2 * LANES // channels
    rows = total // planes
    whole = (total, cells)
    return pl.pallas_call(
        functools.partial(slab_kernel, slab, planes, 16),
        out_shape=(
            pltpu.MemorySpace.HBM(whole, jnp.bfloat16),
            pltpu.MemorySpace.HBM(whole, jnp.bfloat16),
            jax.ShapeDtypeStruct(blocks.shape, jnp.bfloat16),
        ),
        in_specs=[EVERY] * 8,
        out_specs=(ANYWHERE, ANYWHERE, EVERY),
        scratch_shapes=[
            pltpu.VMEM((total, modes), jnp.float32),
            pltpu.VMEM((total, modes), jnp.float32),
            pltpu.VMEM((total, modes), jnp.float32),
            pltpu.VMEM((rows // 2, cells), jnp.float32),
            pltpu.VMEM((rows // 2, cells), jnp.float32),
            pltpu.VMEM((rows, rows), jnp.bfloat16),
            pltpu.VMEM((rows, 1), jnp.float32),
            pltpu.VMEM(whole, jnp.bfloat16),
            pltpu.VMEM(whole, jnp.bfloat16),
            pltpu.SemaphoreType.DMA((2 * planes,)),
            pltpu.SemaphoreType.DMA((2 * planes,)),
        ],
        compiler_params=params(),
        cost_estimate=pl.CostEstimate(flops=4 * total * cells * modes, bytes_accessed=11 << 20, transcendentals=2 * total * cells),
        name="slab_stage",
    )(blocks, field, weight, spread_table(channels, slab), bias, cotangent, synth, table)


def pointwise_kernel(slab, planes, field_ref, weight_ref, spread_ref, out_ref, matrix):
    matrix[...] = mixing_matrix(spread_ref, weight_ref, slab, 0)
    for z in range(planes):
        product = dot(matrix[...], part_of(field_ref, z, planes)[...], ((1,), (0,)))
        part_of(out_ref, z, planes)[...] = product.astype(out_ref.dtype)


def pointwise(field, weight):
    total, cells = field.shape
    channels = weight.shape[0]
    planes = 2 * LANES // channels
    rows = total // planes
    slab = rows // channels
    return pl.pallas_call(
        functools.partial(pointwise_kernel, slab, planes),
        out_shape=jax.ShapeDtypeStruct((total, cells), jnp.bfloat16),
        in_specs=[EVERY] * 3,
        out_specs=EVERY,
        scratch_shapes=[pltpu.VMEM((rows, rows), jnp.bfloat16)],
        compiler_params=params(),
        cost_estimate=pl.CostEstimate(flops=2 * total * rows * cells, bytes_accessed=6 << 20, transcendentals=0),
        name="pointwise",
    )(field, weight, spread_table(channels, slab))


def final_kernel(slab, planes, blocks_ref, through_ref, synth_ref, out_hbm, by_peer, by_rows, out, out_sems):
    blocks_to_rows(blocks_ref, slab, by_peer, by_rows)
    sends = [pltpu.make_async_copy(part_of(out, z, planes), part_of(out_hbm, z, planes), out_sems.at[z]) for z in range(planes)]
    for z in range(planes):
        modal = part_of(by_rows, z, planes)[...].astype(jnp.bfloat16)
        through = part_of(through_ref, z, planes)[...].astype(jnp.float32)
        part_of(out, z, planes)[...] = (dot(modal, synth_ref[...], ((1,), (0,))) + through).astype(out.dtype)
        sends[z].start()
    for send in sends:
        send.wait()


def final_stage(blocks, through, synth):
    total, cells = through.shape
    modes = synth.shape[0]
    slab = total // (2 * LANES)
    planes = 4
    return pl.pallas_call(
        functools.partial(final_kernel, slab, planes),
        out_shape=pltpu.MemorySpace.HBM((total, cells), jnp.bfloat16),
        in_specs=[EVERY] * 3,
        out_specs=ANYWHERE,
        scratch_shapes=[
            pltpu.VMEM((total, modes), jnp.float32),
            pltpu.VMEM((total, modes), jnp.float32),
            pltpu.VMEM((total, cells), jnp.bfloat16),
            pltpu.SemaphoreType.DMA((planes,)),
        ],
        compiler_params=params(),
        cost_estimate=pl.CostEstimate(flops=2 * total * cells * modes, bytes_accessed=7 << 20, transcendentals=0),
        name="final_stage",
    )(blocks, through, synth)


def weight_grad_kernel(step_channels, coeffs_ref, grads_ref, out_ref):
    channels = out_ref.shape[1]
    planes = coeffs_ref.shape[0] // channels
    first = pl.program_id(0) * step_channels

    def step(i, carry):
        total = None
        for z in range(planes):
            row = coeffs_ref[pl.ds(z * channels + first + i, 1), :]
            term = row * grads_ref[z * channels : (z + 1) * channels, :]
            total = term if total is None else total + term
        out_ref[i] = total
        return carry

    lax.fori_loop(0, step_channels, step, 0, unroll=4)


def weight_grad(coeffs, grads, channels):
    modes = coeffs.shape[1]
    step_channels = 16
    fixed = pl.BlockSpec(coeffs.shape, lambda s: (0, 0))
    return pl.pallas_call(
        functools.partial(weight_grad_kernel, step_channels),
        out_shape=jax.ShapeDtypeStruct((channels, channels, modes), jnp.float32),
        grid=(channels // step_channels,),
        in_specs=[fixed, fixed],
        out_specs=pl.BlockSpec((step_channels, channels, modes), lambda s: (s, 0, 0)),
        compiler_params=params(),
        cost_estimate=pl.CostEstimate(flops=2 * coeffs.size * channels, bytes_accessed=5 << 20, transcendentals=0),
        name="weight_grad",
    )(coeffs, grads)


def exchange(blocks, devices):
    tiles = blocks.reshape(devices, blocks.shape[0] // devices, LANES)
    return lax.all_to_all(tiles, AXES, split_axis=0, concat_axis=0, tiled=True).reshape(blocks.shape)


def shards(flow_field, cotangent, spectral_weight, local_weight, channel_bias):
    devices = lax.axis_size("gx") * lax.axis_size("gy")
    planes, channels, slab, cells_along = flow_field.shape
    cells_across = slab * devices
    kept = spectral_weight.shape[3] // 2
    forward_x = basis_table(cells_across, kept, math.sqrt(2.0 / cells_across))
    forward_y = basis_table(cells_along, kept, math.sqrt(2.0 / cells_along))
    inverse_x = basis_table(cells_across, kept, math.sqrt(1.0 / kept))
    inverse_y = basis_table(cells_along, kept, math.sqrt(1.0 / kept))

    def flip(table):
        return jnp.asarray(np.ascontiguousarray(table.T))

    field = flow_field.reshape(planes * channels * slab, cells_along)
    gradient = cotangent.reshape(field.shape)
    weight = spectral_weight.reshape(spectral_weight.shape[1:])
    bias = channel_bias[None, :]

    received = exchange(analysis(field, jnp.asarray(forward_y)), devices)
    modal, coeffs = owner(received, flip(forward_x), jnp.asarray(inverse_x), weight, True)
    gathered = exchange(modal, devices)
    output, grad_pre, grad_rows = slab_stage(
        gathered, field, gradient, local_weight, bias, flip(inverse_y), jnp.asarray(inverse_y)
    )
    received = exchange(grad_rows, devices)
    partial, grads = owner(received, flip(inverse_x), jnp.asarray(forward_x), weight, False)
    gathered = exchange(partial, devices)
    grad_weight = weight_grad(coeffs.astype(jnp.float32), grads.astype(jnp.float32), channels)
    grad_field = final_stage(gathered, pointwise(grad_pre, local_weight), flip(forward_y))
    return (
        output.reshape(flow_field.shape),
        grad_field.reshape(flow_field.shape),
        grad_weight.reshape(spectral_weight.shape),
    )


def solution(mesh):
    placed = (
        P(None, None, AXES, None),
        P(None, None, AXES, None),
        P(AXES, None, None, None),
        P(),
        P(),
    )
    return jax.shard_map(
        shards,
        mesh=mesh,
        in_specs=placed,
        out_specs=(P(None, None, AXES, None), P(None, None, AXES, None), P(AXES, None, None, None)),
        check_vma=False,
    )
```

```python
import functools
import math

import jax
import jax.numpy as jnp
import numpy as np
from jax import lax
from jax.experimental import pallas as pl
from jax.experimental.pallas import tpu as pltpu
from jax.sharding import PartitionSpec as P

AXES = ("gx", "gy")
LANES = 128
VMEM_LIMIT = 20 * 1024 * 1024

ROOT_HALF = 0.7071067811865476
HALF_LOG2E = 0.5 * math.log2(math.e)
DENSITY = 0.3989422804014327


def basis_table(cells, kept, factor):
    positions = np.arange(cells, dtype=np.int64)
    columns = np.arange(2 * kept, dtype=np.int64)
    frequency = np.where(columns < kept, columns, columns - kept + 1)
    phases = positions[:, None] * frequency[None, :] % cells
    angles = phases.astype(np.float32) * np.float32(2.0 * math.pi / cells)
    values = np.where(columns[None, :] < kept, np.cos(angles), np.sin(angles))
    return (values * np.float32(factor)).astype(jnp.bfloat16)


def dot(a, b, contract):
    return lax.dot_general(a, b, (contract, ((), ())), preferred_element_type=jnp.float32)


def in_hbm(array):
    return pltpu.with_memory_space_constraint(array, pltpu.MemorySpace.HBM)


def params():
    return pltpu.CompilerParams(vmem_limit_bytes=VMEM_LIMIT)


def rows_to_blocks(half, slab, by_rows, by_peer):
    tiles = 2 * slab
    for x in range(slab):
        part = by_rows[pl.ds(half * LANES * slab + x, LANES, stride=slab), :]
        by_peer[pl.ds(half * slab + x, LANES, stride=tiles), :] = part.T


def blocks_to_rows(blocks_ref, slab, by_peer, by_rows):
    tiles = 2 * slab
    by_peer[...] = blocks_ref[...].astype(jnp.float32)
    for half in range(2):
        for x in range(slab):
            part = by_peer[pl.ds(half * slab + x, LANES, stride=tiles), :]
            by_rows[pl.ds(half * LANES * slab + x, LANES, stride=slab), :] = part.T


def fetch(pairs, sems):
    copies = [pltpu.make_async_copy(source, target, sems.at[i]) for i, (source, target) in enumerate(pairs)]
    for copy in copies:
        copy.start()
    return copies


def part_of(ref, index, parts):
    rows = ref.shape[0] // parts
    return ref.at[pl.ds(pl.multiple_of(index * rows, rows), rows), :]


def analysis_kernel(slab, pieces, field_hbm, table_hbm, out_ref, by_rows, by_peer, field, table, sems):
    pairs = [(table_hbm, table)]
    pairs += [(part_of(field_hbm, i, 2 * pieces), part_of(field, i, 2 * pieces)) for i in range(pieces)]
    pairs += [(part_of(field_hbm, 1, 2), part_of(field, 1, 2))]
    copies = fetch(pairs, sems)
    for half in range(2):
        for copy in copies[-1:] if half else copies[:-1]:
            copy.wait()
        part_of(by_rows, half, 2)[...] = dot(part_of(field, half, 2)[...], table[...], ((1,), (0,)))
        rows_to_blocks(half, slab, by_rows, by_peer)
    out_ref[...] = by_peer[...].astype(out_ref.dtype)


EVERY = pl.BlockSpec(memory_space=pltpu.VMEM)
ANYWHERE = pl.BlockSpec(memory_space=pl.ANY)


def analysis(field, table):
    total, cells = field.shape
    peers = table.shape[1]
    slab = total // (2 * LANES)
    pieces = 4
    return pl.pallas_call(
        functools.partial(analysis_kernel, slab, pieces),
        out_shape=jax.ShapeDtypeStruct((peers * 2 * slab, LANES), jnp.bfloat16),
        in_specs=[ANYWHERE, ANYWHERE],
        out_specs=EVERY,
        scratch_shapes=[
            pltpu.VMEM((total, peers), jnp.float32),
            pltpu.VMEM((peers * 2 * slab, LANES), jnp.float32),
            pltpu.VMEM(field.shape, field.dtype),
            pltpu.VMEM(table.shape, table.dtype),
            pltpu.SemaphoreType.DMA((2 + pieces,)),
        ],
        compiler_params=params(),
        cost_estimate=pl.CostEstimate(flops=2 * total * cells * peers, bytes_accessed=3 << 20, transcendentals=0),
        name="analysis",
    )(in_hbm(field), in_hbm(table))


def mixing_matrix(spread_ref, weight_ref, slab, axis):
    spread = spread_ref[...]
    wide = dot(spread, weight_ref[...], ((1,), (axis,))).astype(jnp.bfloat16)
    full = dot(wide, spread, ((1,), (1,)))
    row = lax.broadcasted_iota(jnp.int32, full.shape, 0) % slab
    col = lax.broadcasted_iota(jnp.int32, full.shape, 1) % slab
    return jnp.where(row == col, full, 0.0).astype(jnp.bfloat16)


def owner_kernel(forward, slab, blocks_ref, into_ref, back_ref, weight_ref, out_ref, modes_ref, kept, mixed, partial, out, sems):
    peers = blocks_ref.shape[0] // (2 * slab)
    channels = weight_ref.shape[0]
    planes = 2 * LANES // channels
    received = blocks_ref[...].astype(jnp.float32).reshape(peers, 2 * slab, LANES)
    for half in range(2):
        part = received[:, half * slab : (half + 1) * slab, :].reshape(peers * slab, LANES).astype(jnp.bfloat16)
        modes = dot(into_ref[...], part, ((1,), (0,))).T
        kept[half * LANES : (half + 1) * LANES, :] = modes.astype(jnp.bfloat16).astype(jnp.float32)
    modes_ref[...] = kept[...].astype(jnp.bfloat16)
    if forward:

        def step(i, sums):
            weight = weight_ref[i].astype(jnp.float32)
            return tuple(sums[z] + kept[pl.ds(z * channels + i, 1), :] * weight for z in range(planes))

        zeros = jnp.zeros((channels, LANES), jnp.float32)
        sums = lax.fori_loop(0, channels, step, (zeros,) * planes, unroll=16)
        for z in range(planes):
            mixed[z * channels : (z + 1) * channels, :] = sums[z]
    else:

        def step(i, carry):
            weight = weight_ref[i].astype(jnp.float32)
            for z in range(planes):
                product = weight * kept[z * channels : (z + 1) * channels, :]
                folded = product.reshape(channels // 8, 8, LANES).sum(axis=0)
                partial[pl.ds((z * channels + i) * 8, 8), :] = folded
            return carry

        for i in range(channels):
            step(i, 0)
        total = partial[pl.ds(0, planes * channels, stride=8), :]
        for row in range(1, 8):
            total = total + partial[pl.ds(row, planes * channels, stride=8), :]
        mixed[...] = total
    pieces = 1 if forward else 4
    group = peers // pieces
    sent = []
    for i in range(pieces):
        halves = []
        for half in range(2):
            part = mixed[half * LANES : (half + 1) * LANES, :].astype(jnp.bfloat16)
            spatial = dot(back_ref[i * group * slab : (i + 1) * group * slab, :], part, ((1,), (1,)))
            halves.append(spatial.reshape(group, slab, LANES))
        tiles = jnp.concatenate(halves, axis=1).reshape(group * 2 * slab, LANES).astype(out_ref.dtype)
        if forward:
            out_ref[...] = tiles
        else:
            part_of(out, i, pieces)[...] = tiles
            sent.append(pltpu.make_async_copy(part_of(out, i, pieces), part_of(out_ref, i, pieces), sems.at[i]))
            sent[i].start()
    for copy in sent:
        copy.wait()


def owner(blocks, into, back, weight, forward):
    cells, modes = back.shape
    rows = blocks.shape[0]
    channels = weight.shape[0]
    slab = rows // (2 * LANES)
    return pl.pallas_call(
        functools.partial(owner_kernel, forward, slab),
        out_shape=(
            (jax.ShapeDtypeStruct if forward else pltpu.MemorySpace.HBM)(blocks.shape, jnp.bfloat16),
            jax.ShapeDtypeStruct((2 * LANES, modes), jnp.bfloat16),
        ),
        in_specs=[EVERY] * 4,
        out_specs=(EVERY if forward else ANYWHERE, EVERY),
        scratch_shapes=[
            pltpu.VMEM((2 * LANES, modes), jnp.float32),
            pltpu.VMEM((2 * LANES, modes), jnp.float32),
            pltpu.VMEM((8 if forward else 8 * 2 * LANES, modes), jnp.float32),
            pltpu.VMEM((16, LANES) if forward else blocks.shape, jnp.bfloat16),
            pltpu.SemaphoreType.DMA((4,)),
        ],
        compiler_params=params(),
        cost_estimate=pl.CostEstimate(flops=4 * rows * LANES * modes, bytes_accessed=4 << 20, transcendentals=0),
        name="owner_forward" if forward else "owner_backward",
    )(blocks, into, back, weight)


def slab_kernel(slab, planes, chunk, blocks_ref, field_ref, weight_ref, spread_ref, bias_ref, cotangent_ref, synth_ref,
                table_ref, out_hbm, grad_ref, send_ref, by_peer, by_rows, half_rows, pre_even, pre_odd, matrix, offset, out,
                out_sems):
    plane_rows = out.shape[0] // planes
    rows = plane_rows // 2

    def out_copy(i):
        return pltpu.make_async_copy(part_of(out, i, 2 * planes), part_of(out_hbm, i, 2 * planes), out_sems.at[i])

    def fill(target, z, half):
        start = z * plane_rows + half * rows
        modal = by_rows[pl.ds(start, rows), :].astype(jnp.bfloat16)
        mix = matrix[half * rows : (half + 1) * rows, :]
        local = dot(mix, part_of(field_ref, z, planes)[...], ((1,), (0,)))
        target[...] = dot(modal, synth_ref[...], ((1,), (0,))) + local + offset[half * rows : (half + 1) * rows, :]

    def activate(source, z, half):
        start = z * plane_rows + half * rows
        for index in range(rows // chunk):
            there = pl.ds(start + index * chunk, chunk)
            value = source[index * chunk : (index + 1) * chunk, :]
            share = 0.5 + 0.5 * lax.erf(value * ROOT_HALF)
            bell = jnp.exp2(value * value * -HALF_LOG2E)
            out[there, :] = (value * share).astype(out.dtype)
            slope = share + value * bell * DENSITY
            grad_ref[there, :] = (cotangent_ref[there, :].astype(jnp.float32) * slope).astype(grad_ref.dtype)
        out_copy(2 * z + half).start()

    def analyse(z, half):
        here = pl.ds(z * plane_rows + half * rows, rows)
        half_rows[here, :] = dot(grad_ref[here, :], table_ref[...], ((1,), (0,)))

    matrix[...] = mixing_matrix(spread_ref, weight_ref, slab, 1)
    offset[...] = jnp.sum(spread_ref[...].astype(jnp.float32) * bias_ref[...], axis=1, keepdims=True)
    blocks_to_rows(blocks_ref, slab, by_peer, by_rows)
    fill(pre_even, 0, 0)

    def plane(z):
        fill(pre_odd, z, 1)
        activate(pre_even, z, 0)
        analyse(z, 0)
        if z + 1 < planes:
            fill(pre_even, z + 1, 0)
        activate(pre_odd, z, 1)
        analyse(z, 1)

    for z in range(planes):
        plane(z)
    for half in range(2):
        rows_to_blocks(half, slab, half_rows, by_peer)
    send_ref[...] = by_peer[...].astype(send_ref.dtype)
    for i in range(2 * planes):
        out_copy(i).wait()


def spread_table(channels, slab):
    return jnp.asarray(np.kron(np.eye(channels), np.ones((slab, 1))).astype(jnp.bfloat16))


def slab_stage(blocks, field, cotangent, weight, bias, synth, table):
    total, cells = cotangent.shape
    modes = table.shape[1]
    slab = total // (2 * LANES)
    channels = weight.shape[0]
    planes = 2 * LANES // channels
    rows = total // planes
    whole = (total, cells)
    return pl.pallas_call(
        functools.partial(slab_kernel, slab, planes, 16),
        out_shape=(
            pltpu.MemorySpace.HBM(whole, jnp.bfloat16),
            jax.ShapeDtypeStruct(whole, jnp.bfloat16),
            jax.ShapeDtypeStruct(blocks.shape, jnp.bfloat16),
        ),
        in_specs=[EVERY] * 8,
        out_specs=(ANYWHERE, EVERY, EVERY),
        scratch_shapes=[
            pltpu.VMEM((total, modes), jnp.float32),
            pltpu.VMEM((total, modes), jnp.float32),
            pltpu.VMEM((total, modes), jnp.float32),
            pltpu.VMEM((rows // 2, cells), jnp.float32),
            pltpu.VMEM((rows // 2, cells), jnp.float32),
            pltpu.VMEM((rows, rows), jnp.bfloat16),
            pltpu.VMEM((rows, 1), jnp.float32),
            pltpu.VMEM(whole, jnp.bfloat16),
            pltpu.SemaphoreType.DMA((2 * planes,)),
        ],
        compiler_params=params(),
        cost_estimate=pl.CostEstimate(flops=4 * total * cells * modes, bytes_accessed=11 << 20, transcendentals=2 * total * cells),
        name="slab_stage",
    )(blocks, field, weight, spread_table(channels, slab), bias, cotangent, synth, table)


def pointwise_kernel(slab, planes, field_ref, weight_ref, spread_ref, out_ref, matrix, result, sem):
    matrix[...] = mixing_matrix(spread_ref, weight_ref, slab, 0)
    for z in range(planes):
        product = dot(matrix[...], part_of(field_ref, z, planes)[...], ((1,), (0,)))
        part_of(result, z, planes)[...] = product.astype(result.dtype)
    copy = pltpu.make_async_copy(result, out_ref, sem)
    copy.start()
    copy.wait()


def pointwise(field, weight):
    total, cells = field.shape
    channels = weight.shape[0]
    planes = 2 * LANES // channels
    rows = total // planes
    slab = rows // channels
    return pl.pallas_call(
        functools.partial(pointwise_kernel, slab, planes),
        out_shape=jax.ShapeDtypeStruct((total, cells), jnp.bfloat16),
        in_specs=[EVERY] * 3,
        out_specs=EVERY,
        scratch_shapes=[
            pltpu.VMEM((rows, rows), jnp.bfloat16),
            pltpu.VMEM((total, cells), jnp.bfloat16),
            pltpu.SemaphoreType.DMA,
        ],
        input_output_aliases={0: 0},
        compiler_params=params(),
        cost_estimate=pl.CostEstimate(flops=2 * total * rows * cells, bytes_accessed=6 << 20, transcendentals=0),
        name="pointwise",
    )(field, weight, spread_table(channels, slab))


def final_kernel(slab, planes, blocks_ref, through_ref, synth_ref, out_hbm, by_peer, by_rows, out, out_sems):
    blocks_to_rows(blocks_ref, slab, by_peer, by_rows)
    sends = [pltpu.make_async_copy(part_of(out, z, planes), part_of(out_hbm, z, planes), out_sems.at[z]) for z in range(planes)]
    for z in range(planes):
        modal = part_of(by_rows, z, planes)[...].astype(jnp.bfloat16)
        through = part_of(through_ref, z, planes)[...].astype(jnp.float32)
        part_of(out, z, planes)[...] = (dot(modal, synth_ref[...], ((1,), (0,))) + through).astype(out.dtype)
        sends[z].start()
    for send in sends:
        send.wait()


def final_stage(blocks, through, synth):
    total, cells = through.shape
    modes = synth.shape[0]
    slab = total // (2 * LANES)
    planes = 4
    return pl.pallas_call(
        functools.partial(final_kernel, slab, planes),
        out_shape=pltpu.MemorySpace.HBM((total, cells), jnp.bfloat16),
        in_specs=[EVERY] * 3,
        out_specs=ANYWHERE,
        scratch_shapes=[
            pltpu.VMEM((total, modes), jnp.float32),
            pltpu.VMEM((total, modes), jnp.float32),
            pltpu.VMEM((total, cells), jnp.bfloat16),
            pltpu.SemaphoreType.DMA((planes,)),
        ],
        compiler_params=params(),
        cost_estimate=pl.CostEstimate(flops=2 * total * cells * modes, bytes_accessed=7 << 20, transcendentals=0),
        name="final_stage",
    )(blocks, through, synth)


def weight_grad_kernel(step_channels, coeffs_ref, grads_ref, out_ref):
    channels = out_ref.shape[1]
    planes = coeffs_ref.shape[0] // channels
    first = pl.program_id(0) * step_channels

    def step(i, carry):
        total = None
        for z in range(planes):
            row = coeffs_ref[pl.ds(z * channels + first + i, 1), :]
            term = row * grads_ref[z * channels : (z + 1) * channels, :]
            total = term if total is None else total + term
        out_ref[i] = total
        return carry

    lax.fori_loop(0, step_channels, step, 0, unroll=4)


def weight_grad(coeffs, grads, channels):
    modes = coeffs.shape[1]
    step_channels = 16
    fixed = pl.BlockSpec(coeffs.shape, lambda s: (0, 0))
    return pl.pallas_call(
        functools.partial(weight_grad_kernel, step_channels),
        out_shape=jax.ShapeDtypeStruct((channels, channels, modes), jnp.float32),
        grid=(channels // step_channels,),
        in_specs=[fixed, fixed],
        out_specs=pl.BlockSpec((step_channels, channels, modes), lambda s: (s, 0, 0)),
        compiler_params=params(),
        cost_estimate=pl.CostEstimate(flops=2 * coeffs.size * channels, bytes_accessed=5 << 20, transcendentals=0),
        name="weight_grad",
    )(coeffs, grads)


def exchange(blocks, devices):
    tiles = blocks.reshape(devices, blocks.shape[0] // devices, LANES)
    return lax.all_to_all(tiles, AXES, split_axis=0, concat_axis=0, tiled=True).reshape(blocks.shape)


def shards(flow_field, cotangent, spectral_weight, local_weight, channel_bias):
    devices = lax.axis_size("gx") * lax.axis_size("gy")
    planes, channels, slab, cells_along = flow_field.shape
    cells_across = slab * devices
    kept = spectral_weight.shape[3] // 2
    forward_x = basis_table(cells_across, kept, math.sqrt(2.0 / cells_across))
    forward_y = basis_table(cells_along, kept, math.sqrt(2.0 / cells_along))
    inverse_x = basis_table(cells_across, kept, math.sqrt(1.0 / kept))
    inverse_y = basis_table(cells_along, kept, math.sqrt(1.0 / kept))

    def flip(table):
        return jnp.asarray(np.ascontiguousarray(table.T))

    field = flow_field.reshape(planes * channels * slab, cells_along)
    gradient = cotangent.reshape(field.shape)
    weight = spectral_weight.reshape(spectral_weight.shape[1:])
    bias = channel_bias[None, :]

    received = exchange(analysis(field, jnp.asarray(forward_y)), devices)
    modal, coeffs = owner(received, flip(forward_x), jnp.asarray(inverse_x), weight, True)
    gathered = exchange(modal, devices)
    output, grad_pre, grad_rows = slab_stage(
        gathered, field, gradient, local_weight, bias, flip(inverse_y), jnp.asarray(inverse_y)
    )
    received = exchange(grad_rows, devices)
    partial, grads = owner(received, flip(inverse_x), jnp.asarray(forward_x), weight, False)
    gathered = exchange(partial, devices)
    grad_weight = weight_grad(coeffs.astype(jnp.float32), grads.astype(jnp.float32), channels)
    grad_field = final_stage(gathered, pointwise(grad_pre, local_weight), flip(forward_y))
    return (
        output.reshape(flow_field.shape),
        grad_field.reshape(flow_field.shape),
        grad_weight.reshape(spectral_weight.shape),
    )


def solution(mesh):
    placed = (
        P(None, None, AXES, None),
        P(None, None, AXES, None),
        P(AXES, None, None, None),
        P(),
        P(),
    )
    return jax.shard_map(
        shards,
        mesh=mesh,
        in_specs=placed,
        out_specs=(P(None, None, AXES, None), P(None, None, AXES, None), P(AXES, None, None, None)),
        check_vma=False,
    )
```

```python
import functools
import math

import jax
import jax.numpy as jnp
import numpy as np
from jax import lax
from jax.experimental import pallas as pl
from jax.experimental.pallas import tpu as pltpu
from jax.sharding import PartitionSpec as P

AXES = ("gx", "gy")
LANES = 128
VMEM_LIMIT = 20 * 1024 * 1024

ROOT_HALF = 0.7071067811865476
HALF_LOG2E = 0.5 * math.log2(math.e)
DENSITY = 0.3989422804014327


def basis_table(cells, kept, factor):
    positions = np.arange(cells, dtype=np.int64)
    columns = np.arange(2 * kept, dtype=np.int64)
    frequency = np.where(columns < kept, columns, columns - kept + 1)
    phases = positions[:, None] * frequency[None, :] % cells
    angles = phases.astype(np.float32) * np.float32(2.0 * math.pi / cells)
    values = np.where(columns[None, :] < kept, np.cos(angles), np.sin(angles))
    return (values * np.float32(factor)).astype(jnp.bfloat16)


def dot(a, b, contract):
    return lax.dot_general(a, b, (contract, ((), ())), preferred_element_type=jnp.float32)


def in_hbm(array):
    return pltpu.with_memory_space_constraint(array, pltpu.MemorySpace.HBM)


def params():
    return pltpu.CompilerParams(vmem_limit_bytes=VMEM_LIMIT)


def rows_to_blocks(half, slab, by_rows, by_peer):
    tiles = 2 * slab
    for x in range(slab):
        part = by_rows[pl.ds(half * LANES * slab + x, LANES, stride=slab), :]
        by_peer[pl.ds(half * slab + x, LANES, stride=tiles), :] = part.T


def blocks_to_rows(blocks_ref, slab, by_peer, by_rows):
    tiles = 2 * slab
    by_peer[...] = blocks_ref[...].astype(jnp.float32)
    for half in range(2):
        for x in range(slab):
            part = by_peer[pl.ds(half * slab + x, LANES, stride=tiles), :]
            by_rows[pl.ds(half * LANES * slab + x, LANES, stride=slab), :] = part.T


def fetch(pairs, sems):
    copies = [pltpu.make_async_copy(source, target, sems.at[i]) for i, (source, target) in enumerate(pairs)]
    for copy in copies:
        copy.start()
    return copies


def part_of(ref, index, parts):
    rows = ref.shape[0] // parts
    return ref.at[pl.ds(pl.multiple_of(index * rows, rows), rows), :]


def analysis_kernel(slab, pieces, field_hbm, table_hbm, out_ref, by_rows, by_peer, field, table, sems):
    pairs = [(table_hbm, table)]
    pairs += [(part_of(field_hbm, i, 2 * pieces), part_of(field, i, 2 * pieces)) for i in range(pieces)]
    pairs += [(part_of(field_hbm, 1, 2), part_of(field, 1, 2))]
    copies = fetch(pairs, sems)
    for half in range(2):
        for copy in copies[-1:] if half else copies[:-1]:
            copy.wait()
        part_of(by_rows, half, 2)[...] = dot(part_of(field, half, 2)[...], table[...], ((1,), (0,)))
        rows_to_blocks(half, slab, by_rows, by_peer)
    out_ref[...] = by_peer[...].astype(out_ref.dtype)


EVERY = pl.BlockSpec(memory_space=pltpu.VMEM)
ANYWHERE = pl.BlockSpec(memory_space=pl.ANY)


def analysis(field, table):
    total, cells = field.shape
    peers = table.shape[1]
    slab = total // (2 * LANES)
    pieces = 4
    return pl.pallas_call(
        functools.partial(analysis_kernel, slab, pieces),
        out_shape=jax.ShapeDtypeStruct((peers * 2 * slab, LANES), jnp.bfloat16),
        in_specs=[ANYWHERE, ANYWHERE],
        out_specs=EVERY,
        scratch_shapes=[
            pltpu.VMEM((total, peers), jnp.float32),
            pltpu.VMEM((peers * 2 * slab, LANES), jnp.float32),
            pltpu.VMEM(field.shape, field.dtype),
            pltpu.VMEM(table.shape, table.dtype),
            pltpu.SemaphoreType.DMA((2 + pieces,)),
        ],
        compiler_params=params(),
        cost_estimate=pl.CostEstimate(flops=2 * total * cells * peers, bytes_accessed=3 << 20, transcendentals=0),
        name="analysis",
    )(in_hbm(field), in_hbm(table))


def mixing_matrix(spread_ref, weight_ref, slab, axis):
    spread = spread_ref[...]
    wide = dot(spread, weight_ref[...], ((1,), (axis,))).astype(jnp.bfloat16)
    full = dot(wide, spread, ((1,), (1,)))
    row = lax.broadcasted_iota(jnp.int32, full.shape, 0) % slab
    col = lax.broadcasted_iota(jnp.int32, full.shape, 1) % slab
    return jnp.where(row == col, full, 0.0).astype(jnp.bfloat16)


def owner_kernel(forward, slab, blocks_ref, into_ref, back_ref, weight_ref, *refs):
    if forward:
        out_ref, modes_ref, kept, mixed, partial, out, sems = refs
    else:
        waiting_ref, out_ref, modes_ref, stored_ref, kept, mixed, partial, out, sems = refs
        store = pltpu.make_async_copy(waiting_ref, stored_ref, sems.at[4])
        store.start()
    peers = blocks_ref.shape[0] // (2 * slab)
    channels = weight_ref.shape[0]
    planes = 2 * LANES // channels
    received = blocks_ref[...].astype(jnp.float32).reshape(peers, 2 * slab, LANES)
    for half in range(2):
        part = received[:, half * slab : (half + 1) * slab, :].reshape(peers * slab, LANES).astype(jnp.bfloat16)
        modes = dot(into_ref[...], part, ((1,), (0,))).T
        kept[half * LANES : (half + 1) * LANES, :] = modes.astype(jnp.bfloat16).astype(jnp.float32)
    modes_ref[...] = kept[...].astype(jnp.bfloat16)
    if forward:

        def step(i, sums):
            weight = weight_ref[i].astype(jnp.float32)
            return tuple(sums[z] + kept[pl.ds(z * channels + i, 1), :] * weight for z in range(planes))

        zeros = jnp.zeros((channels, LANES), jnp.float32)
        sums = lax.fori_loop(0, channels, step, (zeros,) * planes, unroll=16)
        for z in range(planes):
            mixed[z * channels : (z + 1) * channels, :] = sums[z]
    else:

        def step(i, carry):
            weight = weight_ref[i].astype(jnp.float32)
            for z in range(planes):
                product = weight * kept[z * channels : (z + 1) * channels, :]
                folded = product.reshape(channels // 8, 8, LANES).sum(axis=0)
                partial[pl.ds((z * channels + i) * 8, 8), :] = folded
            return carry

        for i in range(channels):
            step(i, 0)
        total = partial[pl.ds(0, planes * channels, stride=8), :]
        for row in range(1, 8):
            total = total + partial[pl.ds(row, planes * channels, stride=8), :]
        mixed[...] = total
    pieces = 1 if forward else 4
    group = peers // pieces
    sent = []
    for i in range(pieces):
        halves = []
        for half in range(2):
            part = mixed[half * LANES : (half + 1) * LANES, :].astype(jnp.bfloat16)
            spatial = dot(back_ref[i * group * slab : (i + 1) * group * slab, :], part, ((1,), (1,)))
            halves.append(spatial.reshape(group, slab, LANES))
        tiles = jnp.concatenate(halves, axis=1).reshape(group * 2 * slab, LANES).astype(out_ref.dtype)
        if forward:
            out_ref[...] = tiles
        else:
            part_of(out, i, pieces)[...] = tiles
            sent.append(pltpu.make_async_copy(part_of(out, i, pieces), part_of(out_ref, i, pieces), sems.at[i]))
            sent[i].start()
    for copy in sent:
        copy.wait()
    if not forward:
        store.wait()


def owner(blocks, into, back, weight, *waiting):
    forward = not waiting
    cells, modes = back.shape
    rows = blocks.shape[0]
    channels = weight.shape[0]
    slab = rows // (2 * LANES)
    return pl.pallas_call(
        functools.partial(owner_kernel, forward, slab),
        out_shape=(
            (jax.ShapeDtypeStruct if forward else pltpu.MemorySpace.HBM)(blocks.shape, jnp.bfloat16),
            jax.ShapeDtypeStruct((2 * LANES, modes), jnp.bfloat16),
        )
        + tuple(pltpu.MemorySpace.HBM(array.shape, array.dtype) for array in waiting),
        in_specs=[EVERY] * (4 + len(waiting)),
        out_specs=(EVERY if forward else ANYWHERE, EVERY) + (ANYWHERE,) * len(waiting),
        scratch_shapes=[
            pltpu.VMEM((2 * LANES, modes), jnp.float32),
            pltpu.VMEM((2 * LANES, modes), jnp.float32),
            pltpu.VMEM((8 if forward else 8 * 2 * LANES, modes), jnp.float32),
            pltpu.VMEM((16, LANES) if forward else blocks.shape, jnp.bfloat16),
            pltpu.SemaphoreType.DMA((5,)),
        ],
        compiler_params=params(),
        cost_estimate=pl.CostEstimate(flops=4 * rows * LANES * modes, bytes_accessed=4 << 20, transcendentals=0),
        name="owner_forward" if forward else "owner_backward",
    )(blocks, into, back, weight, *waiting)


def slab_kernel(slab, planes, chunk, blocks_ref, field_ref, weight_ref, spread_ref, bias_ref, cotangent_ref, synth_ref,
                table_ref, out, grad_ref, send_ref, by_peer, by_rows, half_rows, pre_even, pre_odd, matrix, offset):
    plane_rows = out.shape[0] // planes
    rows = plane_rows // 2

    def fill(target, z, half):
        start = z * plane_rows + half * rows
        modal = by_rows[pl.ds(start, rows), :].astype(jnp.bfloat16)
        mix = matrix[half * rows : (half + 1) * rows, :]
        local = dot(mix, part_of(field_ref, z, planes)[...], ((1,), (0,)))
        target[...] = dot(modal, synth_ref[...], ((1,), (0,))) + local + offset[half * rows : (half + 1) * rows, :]

    def activate(source, z, half):
        start = z * plane_rows + half * rows
        for index in range(rows // chunk):
            there = pl.ds(start + index * chunk, chunk)
            value = source[index * chunk : (index + 1) * chunk, :]
            share = 0.5 + 0.5 * lax.erf(value * ROOT_HALF)
            bell = jnp.exp2(value * value * -HALF_LOG2E)
            out[there, :] = (value * share).astype(out.dtype)
            slope = share + value * bell * DENSITY
            grad_ref[there, :] = (cotangent_ref[there, :].astype(jnp.float32) * slope).astype(grad_ref.dtype)

    def analyse(z, half):
        here = pl.ds(z * plane_rows + half * rows, rows)
        half_rows[here, :] = dot(grad_ref[here, :], table_ref[...], ((1,), (0,)))

    matrix[...] = mixing_matrix(spread_ref, weight_ref, slab, 1)
    offset[...] = jnp.sum(spread_ref[...].astype(jnp.float32) * bias_ref[...], axis=1, keepdims=True)
    blocks_to_rows(blocks_ref, slab, by_peer, by_rows)
    fill(pre_even, 0, 0)

    def plane(z):
        fill(pre_odd, z, 1)
        activate(pre_even, z, 0)
        analyse(z, 0)
        if z + 1 < planes:
            fill(pre_even, z + 1, 0)
        activate(pre_odd, z, 1)
        analyse(z, 1)

    for z in range(planes):
        plane(z)
    for half in range(2):
        rows_to_blocks(half, slab, half_rows, by_peer)
    send_ref[...] = by_peer[...].astype(send_ref.dtype)


def spread_table(channels, slab):
    return jnp.asarray(np.kron(np.eye(channels), np.ones((slab, 1))).astype(jnp.bfloat16))


def slab_stage(blocks, field, cotangent, weight, bias, synth, table):
    total, cells = cotangent.shape
    modes = table.shape[1]
    slab = total // (2 * LANES)
    channels = weight.shape[0]
    planes = 2 * LANES // channels
    rows = total // planes
    whole = (total, cells)
    return pl.pallas_call(
        functools.partial(slab_kernel, slab, planes, 16),
        out_shape=(
            jax.ShapeDtypeStruct(whole, jnp.bfloat16),
            jax.ShapeDtypeStruct(whole, jnp.bfloat16),
            jax.ShapeDtypeStruct(blocks.shape, jnp.bfloat16),
        ),
        in_specs=[EVERY] * 8,
        out_specs=(EVERY, EVERY, EVERY),
        scratch_shapes=[
            pltpu.VMEM((total, modes), jnp.float32),
            pltpu.VMEM((total, modes), jnp.float32),
            pltpu.VMEM((total, modes), jnp.float32),
            pltpu.VMEM((rows // 2, cells), jnp.float32),
            pltpu.VMEM((rows // 2, cells), jnp.float32),
            pltpu.VMEM((rows, rows), jnp.bfloat16),
            pltpu.VMEM((rows, 1), jnp.float32),
        ],
        compiler_params=params(),
        cost_estimate=pl.CostEstimate(flops=4 * total * cells * modes, bytes_accessed=11 << 20, transcendentals=2 * total * cells),
        name="slab_stage",
    )(blocks, field, weight, spread_table(channels, slab), bias, cotangent, synth, table)


def pointwise_kernel(slab, planes, field_ref, weight_ref, spread_ref, out_ref, matrix, result, sem):
    matrix[...] = mixing_matrix(spread_ref, weight_ref, slab, 0)
    for z in range(planes):
        product = dot(matrix[...], part_of(field_ref, z, planes)[...], ((1,), (0,)))
        part_of(result, z, planes)[...] = product.astype(result.dtype)
    copy = pltpu.make_async_copy(result, out_ref, sem)
    copy.start()
    copy.wait()


def pointwise(field, weight):
    total, cells = field.shape
    channels = weight.shape[0]
    planes = 2 * LANES // channels
    rows = total // planes
    slab = rows // channels
    return pl.pallas_call(
        functools.partial(pointwise_kernel, slab, planes),
        out_shape=jax.ShapeDtypeStruct((total, cells), jnp.bfloat16),
        in_specs=[EVERY] * 3,
        out_specs=EVERY,
        scratch_shapes=[
            pltpu.VMEM((rows, rows), jnp.bfloat16),
            pltpu.VMEM((total, cells), jnp.bfloat16),
            pltpu.SemaphoreType.DMA,
        ],
        input_output_aliases={0: 0},
        compiler_params=params(),
        cost_estimate=pl.CostEstimate(flops=2 * total * rows * cells, bytes_accessed=6 << 20, transcendentals=0),
        name="pointwise",
    )(field, weight, spread_table(channels, slab))


def final_kernel(slab, planes, blocks_ref, through_ref, synth_ref, out_hbm, by_peer, by_rows, out, out_sems):
    blocks_to_rows(blocks_ref, slab, by_peer, by_rows)
    sends = [pltpu.make_async_copy(part_of(out, z, planes), part_of(out_hbm, z, planes), out_sems.at[z]) for z in range(planes)]
    for z in range(planes):
        modal = part_of(by_rows, z, planes)[...].astype(jnp.bfloat16)
        through = part_of(through_ref, z, planes)[...].astype(jnp.float32)
        part_of(out, z, planes)[...] = (dot(modal, synth_ref[...], ((1,), (0,))) + through).astype(out.dtype)
        sends[z].start()
    for send in sends:
        send.wait()


def final_stage(blocks, through, synth):
    total, cells = through.shape
    modes = synth.shape[0]
    slab = total // (2 * LANES)
    planes = 4
    return pl.pallas_call(
        functools.partial(final_kernel, slab, planes),
        out_shape=pltpu.MemorySpace.HBM((total, cells), jnp.bfloat16),
        in_specs=[EVERY] * 3,
        out_specs=ANYWHERE,
        scratch_shapes=[
            pltpu.VMEM((total, modes), jnp.float32),
            pltpu.VMEM((total, modes), jnp.float32),
            pltpu.VMEM((total, cells), jnp.bfloat16),
            pltpu.SemaphoreType.DMA((planes,)),
        ],
        compiler_params=params(),
        cost_estimate=pl.CostEstimate(flops=2 * total * cells * modes, bytes_accessed=7 << 20, transcendentals=0),
        name="final_stage",
    )(blocks, through, synth)


def weight_grad_kernel(step_channels, coeffs_ref, grads_ref, out_ref):
    channels = out_ref.shape[1]
    planes = coeffs_ref.shape[0] // channels
    first = pl.program_id(0) * step_channels

    def step(i, carry):
        total = None
        for z in range(planes):
            row = coeffs_ref[pl.ds(z * channels + first + i, 1), :]
            term = row * grads_ref[z * channels : (z + 1) * channels, :]
            total = term if total is None else total + term
        out_ref[i] = total
        return carry

    lax.fori_loop(0, step_channels, step, 0, unroll=4)


def weight_grad(coeffs, grads, channels):
    modes = coeffs.shape[1]
    step_channels = 16
    fixed = pl.BlockSpec(coeffs.shape, lambda s: (0, 0))
    return pl.pallas_call(
        functools.partial(weight_grad_kernel, step_channels),
        out_shape=jax.ShapeDtypeStruct((channels, channels, modes), jnp.float32),
        grid=(channels // step_channels,),
        in_specs=[fixed, fixed],
        out_specs=pl.BlockSpec((step_channels, channels, modes), lambda s: (s, 0, 0)),
        compiler_params=params(),
        cost_estimate=pl.CostEstimate(flops=2 * coeffs.size * channels, bytes_accessed=5 << 20, transcendentals=0),
        name="weight_grad",
    )(coeffs, grads)


def exchange(blocks, devices):
    tiles = blocks.reshape(devices, blocks.shape[0] // devices, LANES)
    return lax.all_to_all(tiles, AXES, split_axis=0, concat_axis=0, tiled=True).reshape(blocks.shape)


def shards(flow_field, cotangent, spectral_weight, local_weight, channel_bias):
    devices = lax.axis_size("gx") * lax.axis_size("gy")
    planes, channels, slab, cells_along = flow_field.shape
    cells_across = slab * devices
    kept = spectral_weight.shape[3] // 2
    forward_x = basis_table(cells_across, kept, math.sqrt(2.0 / cells_across))
    forward_y = basis_table(cells_along, kept, math.sqrt(2.0 / cells_along))
    inverse_x = basis_table(cells_across, kept, math.sqrt(1.0 / kept))
    inverse_y = basis_table(cells_along, kept, math.sqrt(1.0 / kept))

    def flip(table):
        return jnp.asarray(np.ascontiguousarray(table.T))

    field = flow_field.reshape(planes * channels * slab, cells_along)
    gradient = cotangent.reshape(field.shape)
    weight = spectral_weight.reshape(spectral_weight.shape[1:])
    bias = channel_bias[None, :]

    received = exchange(analysis(field, jnp.asarray(forward_y)), devices)
    modal, coeffs = owner(received, flip(forward_x), jnp.asarray(inverse_x), weight)
    gathered = exchange(modal, devices)
    output, grad_pre, grad_rows = slab_stage(
        gathered, field, gradient, local_weight, bias, flip(inverse_y), jnp.asarray(inverse_y)
    )
    received = exchange(grad_rows, devices)
    partial, grads, output = owner(received, flip(inverse_x), jnp.asarray(forward_x), weight, output)
    gathered = exchange(partial, devices)
    grad_weight = weight_grad(coeffs.astype(jnp.float32), grads.astype(jnp.float32), channels)
    grad_field = final_stage(gathered, pointwise(grad_pre, local_weight), flip(forward_y))
    return (
        output.reshape(flow_field.shape),
        grad_field.reshape(flow_field.shape),
        grad_weight.reshape(spectral_weight.shape),
    )


def solution(mesh):
    placed = (
        P(None, None, AXES, None),
        P(None, None, AXES, None),
        P(AXES, None, None, None),
        P(),
        P(),
    )
    return jax.shard_map(
        shards,
        mesh=mesh,
        in_specs=placed,
        out_specs=(P(None, None, AXES, None), P(None, None, AXES, None), P(AXES, None, None, None)),
        check_vma=False,
    )
```
